32 devices in a mesh: gx: 8 (over z, x), gy: 4 (over y, core).
Axes of the slice: x: 2, y: 2, z: 4, core: 2. Of those that a mesh axis runs over, the one named last changes fastest.
Arguments:
- pressure: float32 [10, 64, 512], P(None, 'gx', 'gy'), may hold values from -3 to 1
- saturation_old: float32 [10, 64, 512], P(None, 'gx', 'gy'), may hold values from 0.3 to 1
- soil_type: int32 [10, 64, 512], P(None, 'gx', 'gy'), may hold values from 0 to 23
- recharge: float32 [64, 512], P('gx', 'gy'), may hold values from -6 to 6
- ksat_table: float32 [24], replicated, may hold values from 0.05 to 5
- alpha_table: float32 [24], replicated, may hold values from 0.3 to 3
- porosity_table: float32 [24], replicated, may hold values from 0.1 to 0.5
- residual_table: float32 [24], replicated, may hold values from 0.02 to 0.3
Outputs:
- pressure_new: float32 [10, 64, 512], P(None, 'gx', 'gy')
The draws below stay inside these ranges and needn't reach their ends.
All inputs are finite; a program needn't handle non-finite values.
Results may differ from the reference program's by a relative error of at most 0.0003.
Values sent between devices are 32-bit elements; how exact they have to be, the bound alone decides.
A program may use at most 64 MiB of HBM per device.

```python
import math
import jax
import jax.numpy as jnp
from jax import lax

NZ = 10
CX = 8
CY = 128
NTYPES = 24
NEWTON = 2
KRYLOV = 2
SWEEPS = 2
COARSE_SWEEPS = 4
NX = 64
NY = 512


def draw_recharge(key, part):
    key = jax.random.fold_in(key, 11)
    level_key, rough_key = jax.random.split(key, 2)
    block_rows = NX // CX
    block_cols = NY // CY
    levels = jnp.exp(jax.random.uniform(level_key, (block_rows, block_cols), jnp.float32, -1.2, 0.6))
    rough_part = jax.random.normal(rough_key, (NX, NY), jnp.float32)
    sign_row = jnp.where(jnp.arange(block_cols) % 2 == 0, 1.0, -1.0).astype(jnp.float32)
    levels = levels * sign_row[None, :]
    smooth_part = jnp.repeat(jnp.repeat(levels, CX, axis=0), CY, axis=1)
    return jnp.clip(smooth_part + rough_part, -6.0, 6.0).astype(jnp.float32)


def with_ends(drawn, rng, low, high):
    dims = drawn.shape
    place = [jax.random.randint(jax.random.fold_in(rng, axis), (), 0, dims[axis]) for axis in range(len(dims))]
    drawn = drawn.at[tuple(place)].set(low)
    longest = dims.index(max(dims))
    place[longest] = (place[longest] + 1) % dims[longest]
    return drawn.at[tuple(place)].set(high)


def steps_of(stream_key, dims, cuts, smallest, top_value):
    loudness, own = 1.0, jax.random.fold_in(stream_key, 6)
    for position, shards_of in cuts:
        steps = jnp.exp(jax.random.uniform(jax.random.fold_in(own, position), (shards_of,), jnp.float32, smallest / len(cuts), top_value / len(cuts)))
        loudness = loudness * jnp.repeat(steps, dims[position] // shards_of).reshape([-1 if axis == position else 1 for axis in range(len(dims))])
    return loudness


def setup_inputs(seed: int = 0) -> dict:
    keys = jax.random.split(jax.random.key(seed), 9)
    pressure = jnp.clip(-3.0 + 4.0 * jax.random.uniform(keys[0], (NZ, NX, NY), jnp.float32) ** steps_of(keys[0], (NZ, NX, NY), ((1, 8), (2, 4)), -0.2, 0.2), -3.0, 1.0)
    saturation_old = jnp.clip(0.3 + 0.7 * jax.random.uniform(keys[1], (NZ, NX, NY), jnp.float32) ** steps_of(keys[1], (NZ, NX, NY), ((1, 8), (2, 4)), -0.2, 0.2), 0.3, 1.0)
    soil_type = with_ends(jax.random.randint(keys[2], (NZ, NX, NY), 0, NTYPES), jax.random.fold_in(keys[2], 1), 0, NTYPES - 1).astype(jnp.int32)
    recharge = draw_recharge(jax.random.fold_in(keys[8], 71), 0)
    ksat_table = jnp.clip(jnp.exp(jax.random.uniform(keys[4], (NTYPES,), jnp.float32, math.log(0.05), math.log(5.0))), 0.05, 5.0)
    alpha_table = jnp.clip(jnp.exp(jax.random.uniform(keys[5], (NTYPES,), jnp.float32, math.log(0.3), math.log(3.0))), 0.3, 3.0)
    porosity_table = jnp.clip(jax.random.uniform(keys[6], (NTYPES,), jnp.float32, 0.1, 0.5), 0.1, 0.5)
    residual_table = jnp.clip(jax.random.uniform(keys[7], (NTYPES,), jnp.float32, 0.02, 0.3), 0.02, 0.3)
    return {"pressure": pressure, "saturation_old": saturation_old, "soil_type": soil_type, "recharge": recharge, "ksat_table": ksat_table, "alpha_table": alpha_table, "porosity_table": porosity_table, "residual_table": residual_table}


OMEGA = 0.8
STORAGE = 0.05
EPSILON = 1e-06

def harmonic(first, second):
    return 2.0 * first * second / (first + second)

def vertical(field):
    zeros_layer = jnp.zeros_like(field[:1])
    return (jnp.concatenate([zeros_layer, field[:-1]], 0), jnp.concatenate([field[1:], zeros_layer], 0))

def neighbours(padded):
    return (padded[:, :-2, 1:-1], padded[:, 2:, 1:-1], padded[:, 1:-1, :-2], padded[:, 1:-1, 2:])

def pad_rim(field):
    return jnp.pad(field, ((0, 0), (1, 1), (1, 1)))

def apply_level(field, padded, coefs):
    storage_term, west_face, east_face, south_face, north_face, lower_face, upper_face = coefs
    west, east, south, north = neighbours(padded)
    below, above = vertical(field)
    return storage_term * field + west_face * (field - west) + east_face * (field - east) + south_face * (field - south) + north_face * (field - north) + lower_face * (field - below) + upper_face * (field - above)

def diagonal_of(coefs):
    storage_term, west_face, east_face, south_face, north_face, lower_face, upper_face = coefs
    return storage_term + west_face + east_face + south_face + north_face + lower_face + upper_face

def blocks(field):
    depth, across, along = field.shape
    return field.reshape(depth, across // 2, 2, along // 2, 2)

def restrict(field):
    parts = blocks(field)
    return parts[:, :, 0, :, 0] + parts[:, :, 0, :, 1] + parts[:, :, 1, :, 0] + parts[:, :, 1, :, 1]

def prolong(field):
    return jnp.repeat(jnp.repeat(field, 2, axis=1), 2, axis=2)

def coarsen(coefs):
    storage_term, west_face, east_face, south_face, north_face, lower_face, upper_face = coefs
    west_parts = blocks(west_face)
    east_parts = blocks(east_face)
    south_parts = blocks(south_face)
    north_parts = blocks(north_face)
    return (restrict(storage_term), west_parts[:, :, 0, :, 0] + west_parts[:, :, 0, :, 1], east_parts[:, :, 1, :, 0] + east_parts[:, :, 1, :, 1], south_parts[:, :, 0, :, 0] + south_parts[:, :, 1, :, 0], north_parts[:, :, 0, :, 1] + north_parts[:, :, 1, :, 1], restrict(lower_face), restrict(upper_face))

def relax(rhs, coefs, diag, sweeps, rim):
    field = OMEGA * rhs / diag
    for sweep in range(sweeps - 1):
        field = field + OMEGA * (rhs - apply_level(field, rim(field), coefs)) / diag
    return field

def resume(field, rhs, coefs, diag, sweeps, rim):
    for sweep in range(sweeps):
        field = field + OMEGA * (rhs - apply_level(field, rim(field), coefs)) / diag
    return field

def vcycle(rhs_fine, level_fine, level_middle, coarse_solve):
    coefs_fine, diag_fine, rim_fine = level_fine
    coefs_middle, diag_middle, rim_middle = level_middle
    fine_iter = relax(rhs_fine, coefs_fine, diag_fine, SWEEPS, rim_fine)
    fine_resid = rhs_fine - apply_level(fine_iter, rim_fine(fine_iter), coefs_fine)
    rhs_middle = restrict(fine_resid)
    middle_iter = relax(rhs_middle, coefs_middle, diag_middle, SWEEPS, rim_middle)
    middle_resid = rhs_middle - apply_level(middle_iter, rim_middle(middle_iter), coefs_middle)
    correction = coarse_solve(restrict(middle_resid))
    middle_iter = resume(middle_iter + prolong(correction), rhs_middle, coefs_middle, diag_middle, SWEEPS, rim_middle)
    fine_iter = resume(fine_iter + prolong(middle_iter), rhs_fine, coefs_fine, diag_fine, SWEEPS, rim_fine)
    return fine_iter

def face_terms(relative, conduct, relative_pad, conduct_pad):
    rel_west, rel_east, rel_south, rel_north = neighbours(relative_pad)
    con_west, con_east, con_south, con_north = neighbours(conduct_pad)
    rel_below, rel_above = vertical(relative)
    con_below, con_above = vertical(conduct)
    return (harmonic(conduct, con_west) * (0.5 * (relative + rel_west)), harmonic(conduct, con_east) * (0.5 * (relative + rel_east)), harmonic(conduct, con_south) * (0.5 * (relative + rel_south)), harmonic(conduct, con_north) * (0.5 * (relative + rel_north)), harmonic(conduct, con_below) * (0.5 * (relative + rel_below)), harmonic(conduct, con_above) * (0.5 * (relative + rel_above)))

def flux_of(state, state_pad, faces):
    west_face, east_face, south_face, north_face, lower_face, upper_face = faces
    west, east, south, north = neighbours(state_pad)
    below, above = vertical(state)
    return west_face * (state - west) + east_face * (state - east) + south_face * (state - south) + north_face * (state - north) + lower_face * (state - below + 1.0) + upper_face * (state - above - 1.0)

def least_squares(hessen, beta, count):
    gram = [[sum((hessen[row][first] * hessen[row][second] for row in range(count + 1))) for second in range(count)] for first in range(count)]
    rhs = [beta * hessen[0][col] for col in range(count)]
    for pivot in range(count):
        for row in range(pivot + 1, count):
            factor = gram[row][pivot] / gram[pivot][pivot]
            for col in range(pivot, count):
                gram[row][col] = gram[row][col] - factor * gram[pivot][col]
            rhs[row] = rhs[row] - factor * rhs[pivot]
    weights = [0.0] * count
    for row in reversed(range(count)):
        total = rhs[row]
        for col in range(row + 1, count):
            total = total - gram[row][col] * weights[col]
        weights[row] = total / gram[row][row]
    return weights

def strip_solver(coefs_coarse, diag_coarse, width):

    def to_strips(field):
        depth, across, along = field.shape
        return field.reshape(depth, across // width, width, along).transpose(1, 0, 2, 3)
    strip_coefs = tuple((to_strips(item) for item in coefs_coarse))
    strip_diag = to_strips(diag_coarse)

    def solve(rhs_coarse):

        def single(rhs_strip, coefs_strip, diag_strip):
            level_mean = lax.optimization_barrier(jnp.sum(rhs_strip, axis=(1, 2))) / lax.optimization_barrier(jnp.sum(coefs_strip[0], axis=(1, 2)))
            start = jnp.zeros_like(rhs_strip) + level_mean[:, None, None]
            return resume(start, rhs_strip, coefs_strip, diag_strip, COARSE_SWEEPS, pad_rim)
        solved = jax.vmap(single)(to_strips(rhs_coarse), strip_coefs, strip_diag)
        return solved.transpose(1, 0, 2, 3).reshape(rhs_coarse.shape)
    return solve

def reference(pressure, saturation_old, soil_type, recharge, ksat_table, alpha_table, porosity_table, residual_table):
    conduct = ksat_table[soil_type]
    alpha = alpha_table[soil_type]
    porosity = porosity_table[soil_type]
    resid = residual_table[soil_type]
    top_layer = lax.broadcasted_iota(jnp.int32, pressure.shape, 0) == pressure.shape[0] - 1
    state = pressure
    for newton_step in range(NEWTON):
        effective = jax.nn.sigmoid(alpha * state)
        saturation = resid + (1.0 - resid) * effective
        slope = (1.0 - resid) * alpha * effective * (1.0 - effective)
        relative = effective * effective
        faces = face_terms(relative, conduct, pad_rim(relative), pad_rim(conduct))
        nonlinear = porosity * (saturation - saturation_old) + STORAGE * (state - pressure) + flux_of(state, pad_rim(state), faces)
        nonlinear = nonlinear - jnp.where(top_layer, recharge[None], 0.0)
        coefs_fine = (STORAGE + porosity * slope,) + faces
        coefs_middle = coarsen(coefs_fine)
        coefs_coarse = coarsen(coefs_middle)
        level_fine = (coefs_fine, diagonal_of(coefs_fine), pad_rim)
        level_middle = (coefs_middle, diagonal_of(coefs_middle), pad_rim)
        coarse_solve = strip_solver(coefs_coarse, diagonal_of(coefs_coarse), CX // 4)
        beta = jnp.sqrt(jnp.sum(nonlinear * nonlinear) + EPSILON)
        basis = [-nonlinear / beta]
        directions = []
        hessen = [[0.0] * KRYLOV for row in range(KRYLOV + 1)]
        for inner in range(KRYLOV):
            direction = vcycle(basis[inner], level_fine, level_middle, coarse_solve)
            directions.append(direction)
            image = apply_level(direction, pad_rim(direction), coefs_fine)
            products = [jnp.sum(vector * image) for vector in basis]
            for index in range(len(basis)):
                hessen[index][inner] = products[index]
                image = image - products[index] * basis[index]
            norm_next = jnp.sqrt(jnp.sum(image * image) + EPSILON)
            hessen[inner + 1][inner] = norm_next
            basis.append(image / norm_next)
        weights = least_squares(hessen, beta, KRYLOV)
        for inner in range(KRYLOV):
            state = state + weights[inner] * directions[inner]
    return state
```

```python
import functools

import jax
import jax.numpy as jnp
from jax import lax
from jax.experimental import pallas as pl
from jax.experimental.pallas import tpu as pltpu
from jax.sharding import PartitionSpec as P

NEWTON = 2
COARSE_SWEEPS = 4
OMEGA = 0.8
STORAGE = 0.05
EPSILON = 1e-06

ROWS = 24
LANES = 256
TILE = (8, 128)
MESH = pl.DeviceIdType.MESH
DIRECTIONS = tuple((dx, dy) for dx in (-1, 0, 1) for dy in (-1, 0, 1) if (dx, dy) != (0, 0))
HALO = 3


def roll(field, shift, axis):
    size = field.shape[axis]
    return pltpu.roll(field, shift % size if isinstance(shift, int) else shift, axis)


def iota(shape, axis):
    return lax.broadcasted_iota(jnp.int32, shape, axis)


def pair(field, step, axis):
    low = (iota(field.shape, axis) & step) == 0
    return jnp.where(low, roll(field, -step, axis), roll(field, step, axis))


def sum_pair(field, step, axis):
    return field + pair(field, step, axis)


def sum_four(field, step):
    return sum_pair(sum_pair(field, step, 1), step, 0)


def spread_low(field, step, axis):
    low = (iota(field.shape, axis) & step) == 0
    return jnp.where(low, field, roll(field, step, axis))


def spread_high(field, step, axis):
    low = (iota(field.shape, axis) & step) == 0
    return jnp.where(low, roll(field, -step, axis), field)


def coarsen(coefs, step):
    storage, west, east, south, north, lower, upper = coefs
    return (
        sum_four(storage, step),
        spread_low(sum_pair(west, step, 1), step, 0),
        spread_high(sum_pair(east, step, 1), step, 0),
        spread_low(sum_pair(south, step, 0), step, 1),
        spread_high(sum_pair(north, step, 0), step, 1),
        sum_four(lower, step),
        sum_four(upper, step),
    )


def kernel(
    gxn, gyn, depth,
    pressure, saturation_old, soil_type, recharge, ksat, alpha_t, porosity_t, residual_t,
    out,
    old, state, sat, con, alp, por, res, rch, rel,
    lev0, lev1, g, b0, xa, xb, b1, ya, yb, z0,
    own, msg0, recv0_w, recv0_e, pack0, recv0_n, recv0_s,
    msg, recv_w, recv_e, pack, recv_n, recv_s,
    msgz, recvz_w, recvz_e, packz, recvz_n, recvz_s,
    coarse_out, coarse_in, rhs_out, rhs_in, strip, strip_sum, solved,
    part_out, part_y, part_x, whole_x,
    s0, r0, sh, rh, sz, rz, sc, rc, sb, rb, sy, ry, sx, rx,
):
    gx, gy = lax.axis_index("gx"), lax.axis_index("gy")
    has_w, has_e = gx > 0, gx < gxn - 1
    has_s, has_n = gy > 0, gy < gyn - 1
    last = depth - 1

    def inside(dx, dy):
        x, y = gx + dx, gy + dy
        return (x >= 0) & (x < gxn) & (y >= 0) & (y < gyn)

    def place(dx, dy):
        return (jnp.clip(gx + dx, 0, gxn - 1), jnp.clip(gy + dy, 0, gyn - 1))

    for ref in (recv0_w, recv0_e, recv0_n, recv0_s, recv_w, recv_e, recv_n, recv_s,
                recvz_w, recvz_e, recvz_n, recvz_s, coarse_in, rhs_in, pack0, pack, packz):
        ref[...] = jnp.zeros(ref.shape, ref.dtype)

    barrier = pltpu.get_barrier_semaphore()
    for dx in (-1, 0, 1):
        for j in range(gyn):
            if (dx, j) != (0, 0):
                @pl.when(inside(dx, 0))
                def _():
                    pl.semaphore_signal(barrier, inc=1, device_id=(jnp.clip(gx + dx, 0, gxn - 1), lax.rem(gy + j, gyn)), device_id_type=MESH)
    for j in range(1, gxn):
        x = lax.rem(gx + j, gxn)
        @pl.when((x != gx - 1) & (x != gx + 1))
        def _():
            pl.semaphore_signal(barrier, inc=1, device_id=(x, gy), device_id_type=MESH)
    strips = 1 + has_w.astype(jnp.int32) + has_e.astype(jnp.int32)
    pl.semaphore_wait(barrier, gyn * strips - 1 + gxn - strips)

    lane8, row8 = iota(TILE, 1), iota(TILE, 0)
    slot8 = (row8 & 3) * 4 + (lane8 & 3)
    lane_e, row_e = iota((ROWS, LANES), 1), iota((ROWS, LANES), 0)
    lane24 = iota((ROWS, 128), 1)
    even_row = (row_e & 1) == 0

    def put_edges(packs, k, block):
        at = lax.rem(k, 16)
        moved = roll(block, at * 8, 1)
        group = lane8 >> 3
        where = k // 16
        packs[0, where] = jnp.where(group == at, moved, packs[0, where])
        packs[1, where] = jnp.where(group == lax.rem(at + 15, 16), moved, packs[1, where])

    def halo_copies(blocks, packs, to_w, to_e, to_n, to_s, send, recv):
        copies = []
        for d, (dx, dy) in enumerate(DIRECTIONS):
            rows = pl.ds(8 * (1 - dx), 8)
            if dy == 0:
                src, dst = blocks, (to_w if dx > 0 else to_e)
            elif dy > 0:
                src, dst = packs.at[1], to_s.at[:, rows]
            else:
                src, dst = packs.at[0], to_n.at[:, rows]
            copy = pltpu.make_async_remote_copy(
                src_ref=src, dst_ref=dst, send_sem=send.at[d], recv_sem=recv.at[d],
                device_id=place(dx, dy), device_id_type=MESH)
            copies.append((copy, inside(dx, dy), inside(-dx, -dy)))
        return copies

    def gather_copies(src, dst, send, recv):
        copies = []
        for dx in (-1, 0, 1):
            for j in range(gyn):
                if (dx, j) == (0, 0):
                    continue
                copy = pltpu.make_async_remote_copy(
                    src_ref=src, dst_ref=dst.at[1 - dx, gy], send_sem=send.at[1 - dx, j], recv_sem=recv.at[1 - dx, j],
                    device_id=(jnp.clip(gx + dx, 0, gxn - 1), lax.rem(gy + j, gyn)), device_id_type=MESH)
                copies.append((copy, inside(dx, 0), inside(-dx, 0)))
        return copies

    def sum_copies(src, dst, send, recv, count, along_x):
        copies = []
        for j in range(1, count):
            to = (lax.rem(gx + j, gxn), gy) if along_x else (gx, lax.rem(gy + j, gyn))
            copy = pltpu.make_async_remote_copy(
                src_ref=src, dst_ref=dst.at[j], send_sem=send.at[j], recv_sem=recv.at[j],
                device_id=to, device_id_type=MESH)
            copies.append((copy, None, None))
        return copies

    def each(copies, do, which):
        for entry in copies:
            if entry[which] is None:
                do(entry[0])
            else:
                @pl.when(entry[which])
                def _():
                    do(entry[0])

    def start(copies):
        each(copies, lambda copy: copy.start(), 1)

    def arrive(copies):
        each(copies, lambda copy: copy.wait_recv(), 2)

    def sent(copies):
        each(copies, lambda copy: copy.wait_send(), 1)

    def extended(k, block, from_w, from_e, from_n, from_s):
        left = jnp.concatenate([from_w[k], block, from_e[k]], axis=0)
        back = lax.rem(16 - lax.rem(k, 16), 16) * 8
        where = k // 16
        north, south = roll(from_n[where], back, 1), roll(from_s[where], back, 1)
        right = jnp.where(lane24 < 8, north, jnp.where(lane24 >= 120, south, 0.0))
        return jnp.concatenate([left, right], axis=1)

    def layers(body, count=depth):
        def step(k, carry):
            body(k)
            return carry
        lax.fori_loop(0, count, step, 0)

    def stage(k):
        msg0[k] = pressure[k]
        msg0[depth + k] = saturation_old[k]
        msg0[2 * depth + k] = soil_type[k].astype(jnp.float32)
    layers(stage)
    msg0[3 * depth] = recharge[...]
    layers(lambda k: put_edges(pack0, k, msg0[k]), 3 * depth + 1)
    first = halo_copies(msg0, pack0, recv0_w, recv0_e, recv0_n, recv0_s, s0, r0)
    start(first)
    arrive(first)

    valid = (
        ((row_e >= 8) | has_w) & ((row_e < 16) | has_e)
        & ((lane_e < 128) | ((lane_e < 136) & has_n) | ((lane_e >= 248) & has_s))
    )

    def first_ext(k):
        return extended(k, msg0[k], recv0_w, recv0_e, recv0_n, recv0_s)

    def unpack_inputs(k):
        old[k] = first_ext(k)
        state[k] = old[k]
        sat[k] = first_ext(depth + k)
        soil = first_ext(2 * depth + k)
        values = [jnp.zeros((ROWS, LANES), jnp.float32) for _ in range(4)]
        for kind in range(ksat.shape[0]):
            here = soil == float(kind)
            values = [jnp.where(here, table[kind], value) for table, value in zip((ksat, alpha_t, porosity_t, residual_t), values)]
        con[k] = jnp.where(valid, values[0], 0.0)
        alp[k], por[k], res[k] = values[1], values[2], values[3]
    layers(unpack_inputs)
    rch[...] = first_ext(3 * depth)
    sent(first)

    def pulled(level, ref, k, field, step):
        total = level[2, k] * roll(field, step, 0) + level[3, k] * roll(field, -step, 0)
        total = total + level[4, k] * roll(field, step, 1) + level[5, k] * roll(field, -step, 1)
        below, above = ref[jnp.maximum(k - 1, 0)], ref[jnp.minimum(k + 1, last)]
        return total + level[6, k] * below + level[7, k] * above

    def residual(level, ref, rhs, k, step):
        field = ref[k]
        return field, rhs[k] - level[0, k] * field + pulled(level, ref, k, field, step)

    def sweep(level, src, rhs, dst, step):
        def body(k):
            field, left = residual(level, src, rhs, k, step)
            dst[k] = field + level[1, k] * left
        layers(body)

    def precondition(nt, j, rhs, gathers, received, first_of_step):
        def begin(k):
            xa[k] = lev0[1, k] * rhs[k]
        layers(begin)
        sweep(lev0, xa, rhs, xb, 1)

        def down(k):
            _, left = residual(lev0, xb, rhs, k, 1)
            total = sum_four(left, 1)
            b1[k] = total
            ya[k] = lev1[1, k] * total
        layers(down)
        sweep(lev1, ya, b1, yb, 2)
        turn = 2 * j

        def deep(k, packed):
            field, left = residual(lev1, yb, b1, k, 2)
            total = sum_four(left[8:16, :128], 2)
            mix = jnp.where((row8 & 1) == 0, field[8:16, :128], b1[k][8:16, :128])
            msg[nt, turn, k] = mix
            put_edges(pack.at[nt, turn], k, mix)
            return jnp.where(slot8 == k, total, packed)
        packed = lax.fori_loop(0, depth, deep, jnp.zeros(TILE, jnp.float32))
        if first_of_step:
            coarse_out[nt, 7] = packed
            coarse_in[nt, 1, gy] = coarse_out[nt]
        else:
            rhs_out[nt] = packed
            rhs_in[nt, 1, gy] = packed
        halo = halo_copies(msg.at[nt, turn], pack.at[nt, turn], recv_w.at[nt, turn], recv_e.at[nt, turn],
                           recv_n.at[nt, turn], recv_s.at[nt, turn], sh.at[nt, turn], rh.at[nt, turn])
        start(gathers)
        start(halo)
        arrive(gathers)

        def strips_of(pick):
            return jnp.concatenate(
                [jnp.concatenate([pick(s, y) for y in range(gyn)], axis=1) for s in range(3)], axis=0)

        width = 128 * gyn
        wide_lane, wide_row = iota((ROWS, width), 1), iota((ROWS, width), 0)

        def strip_totals(field):
            total = field[:, :128]
            for y in range(1, gyn):
                total = total + field[:, 128 * y:128 * (y + 1)]
            for step in (4, 8, 16, 32, 64):
                total = total + roll(total, step, 1)
            return sum_pair(total, 4, 0)

        if first_of_step:
            parts = [strips_of(lambda s, y: coarse_in[nt, s, y, f]) for f in range(7)]
            diag = parts[0]
            for part in parts[1:]:
                diag = diag + part
            live = diag > 0.0
            strip[0] = diag
            strip[1] = jnp.where(live, OMEGA / jnp.where(live, diag, 1.0), 0.0)
            half = (wide_row & 4) == 0
            strip[2] = jnp.where(half, 0.0, parts[1])
            strip[3] = jnp.where(half, parts[2], 0.0)
            for f in range(3, 7):
                strip[f + 1] = parts[f]
            strip_sum[...] = strip_totals(parts[0])
            b2 = strips_of(lambda s, y: coarse_in[nt, s, y, 7])
        else:
            b2 = strips_of(lambda s, y: rhs_in[nt, s, y])
        below_sum = strip_sum[...]
        some = below_sum > 0.0
        mean = jnp.where(some, strip_totals(b2) / jnp.where(some, below_sum, 1.0), 0.0)

        def coarse_sweep(_, e):
            up1, up2 = roll(e, 1, 1), roll(roll(e, 1, 0), -3, 1)
            below = jnp.where((wide_lane & 3) == 0, up2, up1)
            dn1, dn2 = roll(e, -1, 1), roll(roll(e, -1, 0), 3, 1)
            above = jnp.where((wide_lane & 3) == 3, dn2, dn1)
            total = b2 - strip[0] * e
            total = total + strip[2] * roll(e, 4, 0) + strip[3] * roll(e, -4, 0)
            total = total + strip[4] * roll(e, 4, 1) + strip[5] * roll(e, -4, 1)
            total = total + strip[6] * below + strip[7] * above
            return e + strip[1] * total
        e2 = lax.fori_loop(0, COARSE_SWEEPS, coarse_sweep, jnp.concatenate([mean] * gyn, axis=1))
        for y in range(gyn):
            solved[y] = e2[:, 128 * y:128 * (y + 1)]
        right = jnp.where(lane24 < 64, solved[jnp.minimum(gy + 1, gyn - 1)], solved[jnp.maximum(gy - 1, 0)])
        around = jnp.concatenate([solved[gy], right], axis=1)
        slot_e = (row_e & 3) * 4 + (lane_e & 3)
        arrive(halo)

        def up(k):
            m = jnp.where(slot_e == k, around, 0.0)
            m = roll(m, lax.rem(LANES - (k & 3), LANES), 1)
            m = m + roll(m, 1, 1)
            m = m + roll(m, 2, 1)
            m = roll(m, lax.rem(ROWS - (k >> 2), ROWS), 0)
            m = m + roll(m, 1, 0)
            m = m + roll(m, 2, 0)
            mix = extended(k, msg[nt, turn, k], recv_w.at[nt, turn], recv_e.at[nt, turn],
                           recv_n.at[nt, turn], recv_s.at[nt, turn])
            ya[k] = m + jnp.where(even_row, mix, roll(mix, 1, 0))
            b1[k] = jnp.where(even_row, roll(mix, -1, 0), mix)
        layers(up)
        sweep(lev1, ya, b1, yb, 2)

        def join(k):
            field, left = residual(lev1, yb, b1, k, 2)
            xb[k] = xb[k] + field + lev1[1, k] * left
        layers(join)
        sweep(lev0, xb, rhs, xa, 1)
        sweep(lev0, xa, rhs, xb, 1)
        sent(gathers)
        sent(halo)

    def applied(k):
        field = xb[k]
        return (lev0[0, k] * field - pulled(lev0, xb, k, field, 1))[8:16, :128]

    def newton(nt, carry):
        def cells(k):
            effective = 1.0 / (1.0 + jnp.exp(-(alp[k] * state[k])))
            saturation = res[k] + (1.0 - res[k]) * effective
            slope = (1.0 - res[k]) * alp[k] * effective * (1.0 - effective)
            rel[k] = effective * effective
            xa[k] = STORAGE + por[k] * slope
            g[k] = por[k] * (saturation - sat[k]) + STORAGE * (state[k] - old[k])
        layers(cells)

        def faces(k):
            def face(con_n, rel_n):
                total = con[k] + con_n
                live = total > 0.0
                return 2.0 * con[k] * con_n / jnp.where(live, total, 1.0) * (0.5 * (rel[k] + rel_n))
            west = face(roll(con[k], 1, 0), roll(rel[k], 1, 0))
            south = face(roll(con[k], 1, 1), roll(rel[k], 1, 1))
            lower = face(con[jnp.maximum(k - 1, 0)], rel[jnp.maximum(k - 1, 0)])
            lev0[2, k], lev0[3, k] = west, roll(west, -1, 0)
            lev0[4, k], lev0[5, k] = south, roll(south, -1, 1)
            lev0[6, k] = jnp.where(k > 0, lower, 0.0)
        layers(faces)

        def operators(k):
            west, east, south, north, lower = (lev0[f, k] for f in range(2, 7))
            upper = jnp.where(k < last, lev0[6, jnp.minimum(k + 1, last)], 0.0)
            lev0[7, k] = upper
            fine = (xa[k], west, east, south, north, lower, upper)
            diag = fine[0] + west + east + south + north + lower + upper
            lev0[0, k], lev0[1, k] = diag, OMEGA / diag
            here = state[k]
            below, above = state[jnp.maximum(k - 1, 0)], state[jnp.minimum(k + 1, last)]
            flux = (
                west * (here - roll(here, 1, 0)) + east * (here - roll(here, -1, 0))
                + south * (here - roll(here, 1, 1)) + north * (here - roll(here, -1, 1))
                + lower * (here - below + 1.0) + upper * (here - above - 1.0)
            )
            g[k] = jnp.where(k == last, rch[...], 0.0) - g[k] - flux
            middle = coarsen(fine, 1)
            diag = middle[0]
            for f in range(1, 7):
                lev1[f + 1, k] = middle[f]
                diag = diag + middle[f]
            lev1[0, k], lev1[1, k] = diag, OMEGA / diag
            coarse = coarsen([field[8:16, :128] for field in middle], 2)
            for f in range(7):
                coarse_out[nt, f] = jnp.where(slot8 == k, coarse[f], coarse_out[nt, f])
        for f in range(7):
            coarse_out[nt, f] = jnp.zeros(TILE, jnp.float32)
        layers(operators)

        coarse = gather_copies(coarse_out.at[nt], coarse_in.at[nt], sc.at[nt], rc.at[nt])
        precondition(nt, 0, g, coarse, coarse_in, True)

        zeros = jnp.zeros(TILE, jnp.float32)

        def image(k, sums):
            gg, gp, pp = sums
            mine = g[k][8:16, :128]
            diff = applied(k) - mine
            z0[k] = xb[k][8:16, :128]
            msgz[nt, k] = z0[k]
            put_edges(packz.at[nt], k, z0[k])
            own[k] = diff
            msg[nt, 1, k] = diff
            put_edges(pack.at[nt, 1], k, diff)
            return gg + mine * mine, gp + mine * diff, pp + diff * diff
        gg, gp, pp = lax.fori_loop(0, depth, image, (zeros, zeros, zeros))
        halo = halo_copies(msg.at[nt, 1], pack.at[nt, 1], recv_w.at[nt, 1], recv_e.at[nt, 1],
                           recv_n.at[nt, 1], recv_s.at[nt, 1], sh.at[nt, 1], rh.at[nt, 1])
        start(halo)
        arrive(halo)

        def spread(k):
            b0[k] = extended(k, own[k], recv_w.at[nt, 1], recv_e.at[nt, 1], recv_n.at[nt, 1], recv_s.at[nt, 1])
        layers(spread)
        sent(halo)

        right_sides = gather_copies(rhs_out.at[nt], rhs_in.at[nt], sb.at[nt], rb.at[nt])
        precondition(nt, 1, b0, right_sides, rhs_in, False)

        def second(k, sums):
            gs, ps, ss = sums
            mine = g[k][8:16, :128]
            im = applied(k)
            u = xb[k][8:16, :128]
            msgz[nt, depth + k] = u
            put_edges(packz.at[nt], depth + k, u)
            return gs + mine * im, ps + own[k] * im, ss + im * im
        gs, ps, ss = lax.fori_loop(0, depth, second, (zeros, zeros, zeros))

        rows = [jnp.sum(item, axis=0, keepdims=True) for item in (gg, gp, pp, gs, ps, ss)]
        tile = zeros
        for i, item in enumerate(rows):
            tile = jnp.where(row8 == i, jnp.broadcast_to(item, TILE), tile)
        part_out[nt] = tile
        along_y = sum_copies(part_out.at[nt], part_y.at[nt], sy.at[nt], ry.at[nt], gyn, False)
        start(along_y)
        basis = halo_copies(msgz.at[nt], packz.at[nt], recvz_w.at[nt], recvz_e.at[nt],
                            recvz_n.at[nt], recvz_s.at[nt], sz.at[nt], rz.at[nt])

        @pl.when(nt < NEWTON - 1)
        def _():
            start(basis)
        arrive(along_y)
        for j in range(1, gyn):
            tile = tile + part_y[nt, j]
        whole_x[nt] = tile
        along_x = sum_copies(whole_x.at[nt], part_x.at[nt], sx.at[nt], rx.at[nt], gxn, True)
        start(along_x)
        arrive(along_x)
        for j in range(1, gxn):
            tile = tile + part_x[nt, j]
        totals = jnp.broadcast_to(jnp.sum(tile, axis=1, keepdims=True), (8, LANES))
        gg, gp, pp, gs, ps, ss = (totals[i:i + 1] for i in range(6))

        square = gg + EPSILON
        beta = jnp.sqrt(square)
        h00 = (gg + gp) / square
        a = (EPSILON - gp) / square
        vv = jnp.maximum(pp + 2.0 * a * gp + a * a * gg, 0.0)
        h10 = jnp.sqrt(vv / square + EPSILON)
        kappa = 1.0 / (beta * h10)
        gw = gs + a * gp + a * gg
        h01 = kappa / beta * gw
        h11 = kappa * kappa * (ps + a * pp + a * gp + a * gw)
        ww = kappa * kappa * (ss + 2.0 * a * (ps + gs) + a * a * (pp + 2.0 * gp + gg))
        v00 = gg / square
        v11 = kappa * kappa * vv
        v01 = kappa / beta * (gp + a * gg)
        rest = ww - h01 * h01 * (2.0 - v00) - h11 * h11 * (2.0 - v11) + 2.0 * h01 * h11 * v01
        h21_sq = jnp.maximum(rest, 0.0) + EPSILON
        m00 = h00 * h00 + h10 * h10
        m01 = h00 * h01 + h10 * h11
        m11 = h01 * h01 + h11 * h11 + h21_sq
        q0, q1 = beta * h00, beta * h01
        factor = m01 / m00
        y1 = (q1 - factor * q0) / (m11 - factor * m01)
        y0 = (q0 - m01 * y1) / m00
        first_weight = y0 / beta + y1 * kappa * a
        second_weight = y1 * kappa

        @pl.when(nt < NEWTON - 1)
        def _():
            arrive(basis)

            def advance(k):
                z = extended(k, z0[k], recvz_w.at[nt], recvz_e.at[nt], recvz_n.at[nt], recvz_s.at[nt])
                u = extended(depth + k, msgz[nt, depth + k], recvz_w.at[nt], recvz_e.at[nt], recvz_n.at[nt], recvz_s.at[nt])
                state[k] = state[k] + first_weight * z + second_weight * u
            layers(advance)
            sent(basis)

        @pl.when(nt == NEWTON - 1)
        def _():
            def finish(k):
                out[k] = (state[k][8:16, :128] + first_weight[:, :128] * z0[k]
                          + second_weight[:, :128] * msgz[nt, depth + k])
            layers(finish)
        sent(along_y)
        sent(along_x)
        return carry

    lax.fori_loop(0, NEWTON, newton, 0)


def on_device(gxn, gyn, *args):
    depth = args[0].shape[0]

    def vmem(*shape):
        return pltpu.VMEM(shape, jnp.float32)

    def dma(*shape):
        return pltpu.SemaphoreType.DMA(shape)

    ext = vmem(depth, ROWS, LANES)
    level = vmem(8, depth, ROWS, LANES)
    n0 = 3 * depth + 1
    p0 = (n0 + 15) // 16
    pz = (2 * depth + 15) // 16
    scratch = [ext] * 7 + [vmem(ROWS, LANES), ext]
    scratch += [level, level] + [ext] * 7 + [vmem(depth, *TILE)]
    scratch += [
        vmem(depth, *TILE), vmem(n0, *TILE), vmem(n0, *TILE), vmem(n0, *TILE),
        vmem(2, p0, *TILE), vmem(p0, ROWS, 128), vmem(p0, ROWS, 128),
        vmem(NEWTON, HALO, depth, *TILE), vmem(NEWTON, HALO, depth, *TILE), vmem(NEWTON, HALO, depth, *TILE),
        vmem(NEWTON, HALO, 2, 1, *TILE), vmem(NEWTON, HALO, 1, ROWS, 128), vmem(NEWTON, HALO, 1, ROWS, 128),
        vmem(NEWTON, 2 * depth, *TILE), vmem(NEWTON, 2 * depth, *TILE), vmem(NEWTON, 2 * depth, *TILE),
        vmem(NEWTON, 2, pz, *TILE), vmem(NEWTON, pz, ROWS, 128), vmem(NEWTON, pz, ROWS, 128),
        vmem(NEWTON, 8, *TILE), vmem(NEWTON, 3, gyn, 8, *TILE), vmem(NEWTON, *TILE), vmem(NEWTON, 3, gyn, *TILE),
        vmem(8, ROWS, 128 * gyn), vmem(ROWS, 128), vmem(gyn, ROWS, 128),
        vmem(NEWTON, *TILE), vmem(NEWTON, gyn, *TILE), vmem(NEWTON, gxn, *TILE), vmem(NEWTON, *TILE),
        dma(8), dma(8), dma(NEWTON, HALO, 8), dma(NEWTON, HALO, 8), dma(NEWTON, 8), dma(NEWTON, 8),
        dma(NEWTON, 3, gyn), dma(NEWTON, 3, gyn), dma(NEWTON, 3, gyn), dma(NEWTON, 3, gyn),
        dma(NEWTON, gyn), dma(NEWTON, gyn), dma(NEWTON, gxn), dma(NEWTON, gxn),
    ]
    return pl.pallas_call(
        functools.partial(kernel, gxn, gyn, depth),
        out_shape=jax.ShapeDtypeStruct(args[0].shape, jnp.float32),
        in_specs=[pl.BlockSpec(memory_space=pltpu.VMEM)] * 4 + [pl.BlockSpec(memory_space=pltpu.SMEM)] * 4,
        out_specs=pl.BlockSpec(memory_space=pltpu.VMEM),
        scratch_shapes=scratch,
        compiler_params=pltpu.CompilerParams(
            collective_id=0, has_side_effects=True, vmem_limit_bytes=40 * 1024 * 1024),
    )(*args)


def solution(mesh):
    cells = P(None, "gx", "gy")
    placed = (cells, cells, cells, P("gx", "gy"), P(), P(), P(), P())
    return jax.shard_map(
        functools.partial(on_device, mesh.shape["gx"], mesh.shape["gy"]),
        mesh=mesh, in_specs=placed, out_specs=cells, check_vma=False,
    )
```

```python
import functools

import jax
import jax.numpy as jnp
from jax import lax
from jax.experimental import pallas as pl
from jax.experimental.pallas import tpu as pltpu
from jax.sharding import PartitionSpec as P

NEWTON = 2
COARSE_SWEEPS = 4
OMEGA = 0.8
STORAGE = 0.05
EPSILON = 1e-06

ROWS = 24
LANES = 256
TILE = (8, 128)
MESH = pl.DeviceIdType.MESH
DIRECTIONS = tuple((dx, dy) for dx in (-1, 0, 1) for dy in (-1, 0, 1) if (dx, dy) != (0, 0))
HALO = 3


def roll(field, shift, axis):
    size = field.shape[axis]
    return pltpu.roll(field, shift % size if isinstance(shift, int) else shift, axis)


def iota(shape, axis):
    return lax.broadcasted_iota(jnp.int32, shape, axis)


def pair(field, step, axis):
    low = (iota(field.shape, axis) & step) == 0
    return jnp.where(low, roll(field, -step, axis), roll(field, step, axis))


def sum_pair(field, step, axis):
    return field + pair(field, step, axis)


def sum_four(field, step):
    return sum_pair(sum_pair(field, step, 1), step, 0)


def spread_low(field, step, axis):
    low = (iota(field.shape, axis) & step) == 0
    return jnp.where(low, field, roll(field, step, axis))


def spread_high(field, step, axis):
    low = (iota(field.shape, axis) & step) == 0
    return jnp.where(low, roll(field, -step, axis), field)


def coarsen(coefs, step):
    storage, west, east, south, north, lower, upper = coefs
    return (
        sum_four(storage, step),
        spread_low(sum_pair(west, step, 1), step, 0),
        spread_high(sum_pair(east, step, 1), step, 0),
        spread_low(sum_pair(south, step, 0), step, 1),
        spread_high(sum_pair(north, step, 0), step, 1),
        sum_four(lower, step),
        sum_four(upper, step),
    )


def kernel(
    gxn, gyn, depth,
    pressure, saturation_old, soil_type, recharge, ksat, alpha_t, porosity_t, residual_t,
    out,
    old, state, sat, con, alp, por, res, rch, rel,
    lev0, lev1, g, b0, xa, xb, b1, ya, yb, z0,
    own, msg0, recv0_w, recv0_e, pack0, recv0_n, recv0_s,
    msg, recv_w, recv_e, pack, recv_n, recv_s,
    msgz, recvz_w, recvz_e, packz, recvz_n, recvz_s,
    coarse_out, coarse_in, rhs_out, rhs_in, strip, strip_sum, solved,
    part_out, part_y, part_x, whole_x,
    s0, r0, sh, rh, sz, rz, sc, rc, sb, rb, sy, ry, sx, rx,
):
    gx, gy = lax.axis_index("gx"), lax.axis_index("gy")
    has_w, has_e = gx > 0, gx < gxn - 1
    has_s, has_n = gy > 0, gy < gyn - 1
    last = depth - 1

    def inside(dx, dy):
        x, y = gx + dx, gy + dy
        return (x >= 0) & (x < gxn) & (y >= 0) & (y < gyn)

    def place(dx, dy):
        return (jnp.clip(gx + dx, 0, gxn - 1), jnp.clip(gy + dy, 0, gyn - 1))

    for ref in (recv0_w, recv0_e, recv0_n, recv0_s, recv_w, recv_e, recv_n, recv_s,
                recvz_w, recvz_e, recvz_n, recvz_s, coarse_in, rhs_in, pack0, pack, packz):
        ref[...] = jnp.zeros(ref.shape, ref.dtype)

    barrier = pltpu.get_barrier_semaphore()
    for dx in (-1, 0, 1):
        for j in range(gyn):
            if (dx, j) != (0, 0):
                @pl.when(inside(dx, 0))
                def _():
                    pl.semaphore_signal(barrier, inc=1, device_id=(jnp.clip(gx + dx, 0, gxn - 1), lax.rem(gy + j, gyn)), device_id_type=MESH)
    for j in range(1, gxn):
        x = lax.rem(gx + j, gxn)
        @pl.when((x != gx - 1) & (x != gx + 1))
        def _():
            pl.semaphore_signal(barrier, inc=1, device_id=(x, gy), device_id_type=MESH)
    strips = 1 + has_w.astype(jnp.int32) + has_e.astype(jnp.int32)
    pl.semaphore_wait(barrier, gyn * strips - 1 + gxn - strips)

    lane8, row8 = iota(TILE, 1), iota(TILE, 0)
    slot8 = (row8 & 3) * 4 + (lane8 & 3)
    lane_e, row_e = iota((ROWS, LANES), 1), iota((ROWS, LANES), 0)
    lane24 = iota((ROWS, 128), 1)
    even_row = (row_e & 1) == 0

    def put_edges(packs, k, block):
        at = lax.rem(k, 16)
        moved = roll(block, at * 8, 1)
        group = lane8 >> 3
        where = k // 16
        packs[0, where] = jnp.where(group == at, moved, packs[0, where])
        packs[1, where] = jnp.where(group == lax.rem(at + 15, 16), moved, packs[1, where])

    def halo_copies(blocks, packs, to_w, to_e, to_n, to_s, send, recv):
        copies = []
        for d, (dx, dy) in enumerate(DIRECTIONS):
            rows = pl.ds(8 * (1 - dx), 8)
            if dy == 0:
                src, dst = blocks, (to_w if dx > 0 else to_e)
            elif dy > 0:
                src, dst = packs.at[1], to_s.at[:, rows]
            else:
                src, dst = packs.at[0], to_n.at[:, rows]
            copy = pltpu.make_async_remote_copy(
                src_ref=src, dst_ref=dst, send_sem=send.at[d], recv_sem=recv.at[d],
                device_id=place(dx, dy), device_id_type=MESH)
            copies.append((copy, inside(dx, dy), inside(-dx, -dy)))
        return copies

    def gather_copies(src, dst, send, recv):
        copies = []
        for dx in (-1, 0, 1):
            for j in range(gyn):
                if (dx, j) == (0, 0):
                    continue
                copy = pltpu.make_async_remote_copy(
                    src_ref=src, dst_ref=dst.at[1 - dx, gy], send_sem=send.at[1 - dx, j], recv_sem=recv.at[1 - dx, j],
                    device_id=(jnp.clip(gx + dx, 0, gxn - 1), lax.rem(gy + j, gyn)), device_id_type=MESH)
                copies.append((copy, inside(dx, 0), inside(-dx, 0)))
        return copies

    def sum_copies(src, dst, send, recv, count, along_x):
        copies = []
        for j in range(1, count):
            to = (lax.rem(gx + j, gxn), gy) if along_x else (gx, lax.rem(gy + j, gyn))
            copy = pltpu.make_async_remote_copy(
                src_ref=src, dst_ref=dst.at[j], send_sem=send.at[j], recv_sem=recv.at[j],
                device_id=to, device_id_type=MESH)
            copies.append((copy, None, None))
        return copies

    def each(copies, do, which):
        for entry in copies:
            if entry[which] is None:
                do(entry[0])
            else:
                @pl.when(entry[which])
                def _():
                    do(entry[0])

    def start(copies):
        each(copies, lambda copy: copy.start(), 1)

    def arrive(copies):
        each(copies, lambda copy: copy.wait_recv(), 2)

    def sent(copies):
        each(copies, lambda copy: copy.wait_send(), 1)

    def extended(k, block, from_w, from_e, from_n, from_s):
        left = jnp.concatenate([from_w[k], block, from_e[k]], axis=0)
        back = lax.rem(16 - lax.rem(k, 16), 16) * 8
        where = k // 16
        north, south = roll(from_n[where], back, 1), roll(from_s[where], back, 1)
        right = jnp.where(lane24 < 8, north, jnp.where(lane24 >= 120, south, 0.0))
        return jnp.concatenate([left, right], axis=1)

    def layers(body, count=depth):
        def step(k, carry):
            body(k)
            return carry
        lax.fori_loop(0, count, step, 0, unroll=True)

    def stage(k):
        msg0[k] = pressure[k]
        msg0[depth + k] = saturation_old[k]
        msg0[2 * depth + k] = soil_type[k].astype(jnp.float32)
    layers(stage)
    msg0[3 * depth] = recharge[...]
    layers(lambda k: put_edges(pack0, k, msg0[k]), 3 * depth + 1)
    first = halo_copies(msg0, pack0, recv0_w, recv0_e, recv0_n, recv0_s, s0, r0)
    start(first)
    arrive(first)

    valid = (
        ((row_e >= 8) | has_w) & ((row_e < 16) | has_e)
        & ((lane_e < 128) | ((lane_e < 136) & has_n) | ((lane_e >= 248) & has_s))
    )

    def first_ext(k):
        return extended(k, msg0[k], recv0_w, recv0_e, recv0_n, recv0_s)

    def unpack_inputs(k):
        old[k] = first_ext(k)
        state[k] = old[k]
        sat[k] = first_ext(depth + k)
        soil = first_ext(2 * depth + k)
        values = [jnp.zeros((ROWS, LANES), jnp.float32) for _ in range(4)]
        for kind in range(ksat.shape[0]):
            here = soil == float(kind)
            values = [jnp.where(here, table[kind], value) for table, value in zip((ksat, alpha_t, porosity_t, residual_t), values)]
        con[k] = jnp.where(valid, values[0], 0.0)
        alp[k], por[k], res[k] = values[1], values[2], values[3]
    layers(unpack_inputs)
    rch[...] = first_ext(3 * depth)
    sent(first)

    def pulled(level, ref, k, field, step):
        total = level[2, k] * roll(field, step, 0) + level[3, k] * roll(field, -step, 0)
        total = total + level[4, k] * roll(field, step, 1) + level[5, k] * roll(field, -step, 1)
        below, above = ref[jnp.maximum(k - 1, 0)], ref[jnp.minimum(k + 1, last)]
        return total + level[6, k] * below + level[7, k] * above

    def residual(level, ref, rhs, k, step):
        field = ref[k]
        return field, rhs[k] - level[0, k] * field + pulled(level, ref, k, field, step)

    def sweep(level, src, rhs, dst, step):
        def body(k):
            field, left = residual(level, src, rhs, k, step)
            dst[k] = field + level[1, k] * left
        layers(body)

    def precondition(nt, j, rhs, gathers, received, first_of_step):
        def begin(k):
            xa[k] = lev0[1, k] * rhs[k]
        layers(begin)
        sweep(lev0, xa, rhs, xb, 1)

        def down(k):
            _, left = residual(lev0, xb, rhs, k, 1)
            total = sum_four(left, 1)
            b1[k] = total
            ya[k] = lev1[1, k] * total
        layers(down)
        sweep(lev1, ya, b1, yb, 2)
        turn = 2 * j

        def deep(k, packed):
            field, left = residual(lev1, yb, b1, k, 2)
            total = sum_four(left[8:16, :128], 2)
            mix = jnp.where((row8 & 1) == 0, field[8:16, :128], b1[k][8:16, :128])
            msg[nt, turn, k] = mix
            put_edges(pack.at[nt, turn], k, mix)
            return jnp.where(slot8 == k, total, packed)
        packed = lax.fori_loop(0, depth, deep, jnp.zeros(TILE, jnp.float32), unroll=True)
        if first_of_step:
            coarse_out[nt, 7] = packed
            coarse_in[nt, 1, gy] = coarse_out[nt]
        else:
            rhs_out[nt] = packed
            rhs_in[nt, 1, gy] = packed
        halo = halo_copies(msg.at[nt, turn], pack.at[nt, turn], recv_w.at[nt, turn], recv_e.at[nt, turn],
                           recv_n.at[nt, turn], recv_s.at[nt, turn], sh.at[nt, turn], rh.at[nt, turn])
        start(gathers)
        start(halo)
        arrive(gathers)

        def strips_of(pick):
            return jnp.concatenate(
                [jnp.concatenate([pick(s, y) for y in range(gyn)], axis=1) for s in range(3)], axis=0)

        width = 128 * gyn
        wide_lane, wide_row = iota((ROWS, width), 1), iota((ROWS, width), 0)

        def strip_totals(field):
            total = field[:, :128]
            for y in range(1, gyn):
                total = total + field[:, 128 * y:128 * (y + 1)]
            for step in (4, 8, 16, 32, 64):
                total = total + roll(total, step, 1)
            return sum_pair(total, 4, 0)

        if first_of_step:
            parts = [strips_of(lambda s, y: coarse_in[nt, s, y, f]) for f in range(7)]
            diag = parts[0]
            for part in parts[1:]:
                diag = diag + part
            live = diag > 0.0
            strip[0] = diag
            strip[1] = jnp.where(live, OMEGA / jnp.where(live, diag, 1.0), 0.0)
            half = (wide_row & 4) == 0
            strip[2] = jnp.where(half, 0.0, parts[1])
            strip[3] = jnp.where(half, parts[2], 0.0)
            for f in range(3, 7):
                strip[f + 1] = parts[f]
            strip_sum[...] = strip_totals(parts[0])
            b2 = strips_of(lambda s, y: coarse_in[nt, s, y, 7])
        else:
            b2 = strips_of(lambda s, y: rhs_in[nt, s, y])
        below_sum = strip_sum[...]
        some = below_sum > 0.0
        mean = jnp.where(some, strip_totals(b2) / jnp.where(some, below_sum, 1.0), 0.0)

        def coarse_sweep(_, e):
            up1, up2 = roll(e, 1, 1), roll(roll(e, 1, 0), -3, 1)
            below = jnp.where((wide_lane & 3) == 0, up2, up1)
            dn1, dn2 = roll(e, -1, 1), roll(roll(e, -1, 0), 3, 1)
            above = jnp.where((wide_lane & 3) == 3, dn2, dn1)
            total = b2 - strip[0] * e
            total = total + strip[2] * roll(e, 4, 0) + strip[3] * roll(e, -4, 0)
            total = total + strip[4] * roll(e, 4, 1) + strip[5] * roll(e, -4, 1)
            total = total + strip[6] * below + strip[7] * above
            return e + strip[1] * total
        e2 = lax.fori_loop(0, COARSE_SWEEPS, coarse_sweep, jnp.concatenate([mean] * gyn, axis=1), unroll=True)
        for y in range(gyn):
            solved[y] = e2[:, 128 * y:128 * (y + 1)]
        right = jnp.where(lane24 < 64, solved[jnp.minimum(gy + 1, gyn - 1)], solved[jnp.maximum(gy - 1, 0)])
        around = jnp.concatenate([solved[gy], right], axis=1)
        slot_e = (row_e & 3) * 4 + (lane_e & 3)
        arrive(halo)

        def up(k):
            m = jnp.where(slot_e == k, around, 0.0)
            m = roll(m, lax.rem(LANES - (k & 3), LANES), 1)
            m = m + roll(m, 1, 1)
            m = m + roll(m, 2, 1)
            m = roll(m, lax.rem(ROWS - (k >> 2), ROWS), 0)
            m = m + roll(m, 1, 0)
            m = m + roll(m, 2, 0)
            mix = extended(k, msg[nt, turn, k], recv_w.at[nt, turn], recv_e.at[nt, turn],
                           recv_n.at[nt, turn], recv_s.at[nt, turn])
            ya[k] = m + jnp.where(even_row, mix, roll(mix, 1, 0))
            b1[k] = jnp.where(even_row, roll(mix, -1, 0), mix)
        layers(up)
        sweep(lev1, ya, b1, yb, 2)

        def join(k):
            field, left = residual(lev1, yb, b1, k, 2)
            xb[k] = xb[k] + field + lev1[1, k] * left
        layers(join)
        sweep(lev0, xb, rhs, xa, 1)
        sweep(lev0, xa, rhs, xb, 1)
        sent(gathers)
        sent(halo)

    def applied(k):
        field = xb[k]
        return (lev0[0, k] * field - pulled(lev0, xb, k, field, 1))[8:16, :128]

    def newton(nt, carry):
        def cells(k):
            effective = 1.0 / (1.0 + jnp.exp(-(alp[k] * state[k])))
            saturation = res[k] + (1.0 - res[k]) * effective
            slope = (1.0 - res[k]) * alp[k] * effective * (1.0 - effective)
            rel[k] = effective * effective
            xa[k] = STORAGE + por[k] * slope
            g[k] = por[k] * (saturation - sat[k]) + STORAGE * (state[k] - old[k])
        layers(cells)

        def faces(k):
            def face(con_n, rel_n):
                total = con[k] + con_n
                live = total > 0.0
                return 2.0 * con[k] * con_n / jnp.where(live, total, 1.0) * (0.5 * (rel[k] + rel_n))
            west = face(roll(con[k], 1, 0), roll(rel[k], 1, 0))
            south = face(roll(con[k], 1, 1), roll(rel[k], 1, 1))
            lower = face(con[jnp.maximum(k - 1, 0)], rel[jnp.maximum(k - 1, 0)])
            lev0[2, k], lev0[3, k] = west, roll(west, -1, 0)
            lev0[4, k], lev0[5, k] = south, roll(south, -1, 1)
            lev0[6, k] = jnp.where(k > 0, lower, 0.0)
        layers(faces)

        def operators(k):
            west, east, south, north, lower = (lev0[f, k] for f in range(2, 7))
            upper = jnp.where(k < last, lev0[6, jnp.minimum(k + 1, last)], 0.0)
            lev0[7, k] = upper
            fine = (xa[k], west, east, south, north, lower, upper)
            diag = fine[0] + west + east + south + north + lower + upper
            lev0[0, k], lev0[1, k] = diag, OMEGA / diag
            here = state[k]
            below, above = state[jnp.maximum(k - 1, 0)], state[jnp.minimum(k + 1, last)]
            flux = (
                west * (here - roll(here, 1, 0)) + east * (here - roll(here, -1, 0))
                + south * (here - roll(here, 1, 1)) + north * (here - roll(here, -1, 1))
                + lower * (here - below + 1.0) + upper * (here - above - 1.0)
            )
            g[k] = jnp.where(k == last, rch[...], 0.0) - g[k] - flux
            middle = coarsen(fine, 1)
            diag = middle[0]
            for f in range(1, 7):
                lev1[f + 1, k] = middle[f]
                diag = diag + middle[f]
            lev1[0, k], lev1[1, k] = diag, OMEGA / diag
            coarse = coarsen([field[8:16, :128] for field in middle], 2)
            for f in range(7):
                coarse_out[nt, f] = jnp.where(slot8 == k, coarse[f], coarse_out[nt, f])
        for f in range(7):
            coarse_out[nt, f] = jnp.zeros(TILE, jnp.float32)
        layers(operators)

        coarse = gather_copies(coarse_out.at[nt], coarse_in.at[nt], sc.at[nt], rc.at[nt])
        precondition(nt, 0, g, coarse, coarse_in, True)

        zeros = jnp.zeros(TILE, jnp.float32)

        def image(k, sums):
            gg, gp, pp = sums
            mine = g[k][8:16, :128]
            diff = applied(k) - mine
            z0[k] = xb[k][8:16, :128]
            msgz[nt, k] = z0[k]
            put_edges(packz.at[nt], k, z0[k])
            own[k] = diff
            msg[nt, 1, k] = diff
            put_edges(pack.at[nt, 1], k, diff)
            return gg + mine * mine, gp + mine * diff, pp + diff * diff
        gg, gp, pp = lax.fori_loop(0, depth, image, (zeros, zeros, zeros), unroll=True)
        halo = halo_copies(msg.at[nt, 1], pack.at[nt, 1], recv_w.at[nt, 1], recv_e.at[nt, 1],
                           recv_n.at[nt, 1], recv_s.at[nt, 1], sh.at[nt, 1], rh.at[nt, 1])
        start(halo)
        arrive(halo)

        def spread(k):
            b0[k] = extended(k, own[k], recv_w.at[nt, 1], recv_e.at[nt, 1], recv_n.at[nt, 1], recv_s.at[nt, 1])
        layers(spread)
        sent(halo)

        right_sides = gather_copies(rhs_out.at[nt], rhs_in.at[nt], sb.at[nt], rb.at[nt])
        precondition(nt, 1, b0, right_sides, rhs_in, False)

        def second(k, sums):
            gs, ps, ss = sums
            mine = g[k][8:16, :128]
            im = applied(k)
            u = xb[k][8:16, :128]
            msgz[nt, depth + k] = u
            put_edges(packz.at[nt], depth + k, u)
            return gs + mine * im, ps + own[k] * im, ss + im * im
        gs, ps, ss = lax.fori_loop(0, depth, second, (zeros, zeros, zeros), unroll=True)

        rows = [jnp.sum(item, axis=0, keepdims=True) for item in (gg, gp, pp, gs, ps, ss)]
        tile = zeros
        for i, item in enumerate(rows):
            tile = jnp.where(row8 == i, jnp.broadcast_to(item, TILE), tile)
        part_out[nt] = tile
        along_y = sum_copies(part_out.at[nt], part_y.at[nt], sy.at[nt], ry.at[nt], gyn, False)
        start(along_y)
        basis = halo_copies(msgz.at[nt], packz.at[nt], recvz_w.at[nt], recvz_e.at[nt],
                            recvz_n.at[nt], recvz_s.at[nt], sz.at[nt], rz.at[nt])

        @pl.when(nt < NEWTON - 1)
        def _():
            start(basis)
        arrive(along_y)
        for j in range(1, gyn):
            tile = tile + part_y[nt, j]
        whole_x[nt] = tile
        along_x = sum_copies(whole_x.at[nt], part_x.at[nt], sx.at[nt], rx.at[nt], gxn, True)
        start(along_x)
        arrive(along_x)
        for j in range(1, gxn):
            tile = tile + part_x[nt, j]
        totals = jnp.broadcast_to(jnp.sum(tile, axis=1, keepdims=True), (8, LANES))
        gg, gp, pp, gs, ps, ss = (totals[i:i + 1] for i in range(6))

        square = gg + EPSILON
        beta = jnp.sqrt(square)
        h00 = (gg + gp) / square
        a = (EPSILON - gp) / square
        vv = jnp.maximum(pp + 2.0 * a * gp + a * a * gg, 0.0)
        h10 = jnp.sqrt(vv / square + EPSILON)
        kappa = 1.0 / (beta * h10)
        gw = gs + a * gp + a * gg
        h01 = kappa / beta * gw
        h11 = kappa * kappa * (ps + a * pp + a * gp + a * gw)
        ww = kappa * kappa * (ss + 2.0 * a * (ps + gs) + a * a * (pp + 2.0 * gp + gg))
        v00 = gg / square
        v11 = kappa * kappa * vv
        v01 = kappa / beta * (gp + a * gg)
        rest = ww - h01 * h01 * (2.0 - v00) - h11 * h11 * (2.0 - v11) + 2.0 * h01 * h11 * v01
        h21_sq = jnp.maximum(rest, 0.0) + EPSILON
        m00 = h00 * h00 + h10 * h10
        m01 = h00 * h01 + h10 * h11
        m11 = h01 * h01 + h11 * h11 + h21_sq
        q0, q1 = beta * h00, beta * h01
        factor = m01 / m00
        y1 = (q1 - factor * q0) / (m11 - factor * m01)
        y0 = (q0 - m01 * y1) / m00
        first_weight = y0 / beta + y1 * kappa * a
        second_weight = y1 * kappa

        @pl.when(nt < NEWTON - 1)
        def _():
            arrive(basis)

            def advance(k):
                z = extended(k, z0[k], recvz_w.at[nt], recvz_e.at[nt], recvz_n.at[nt], recvz_s.at[nt])
                u = extended(depth + k, msgz[nt, depth + k], recvz_w.at[nt], recvz_e.at[nt], recvz_n.at[nt], recvz_s.at[nt])
                state[k] = state[k] + first_weight * z + second_weight * u
            layers(advance)
            sent(basis)

        @pl.when(nt == NEWTON - 1)
        def _():
            def finish(k):
                out[k] = (state[k][8:16, :128] + first_weight[:, :128] * z0[k]
                          + second_weight[:, :128] * msgz[nt, depth + k])
            layers(finish)
        sent(along_y)
        sent(along_x)
        return carry

    lax.fori_loop(0, NEWTON, newton, 0)


def on_device(gxn, gyn, *args):
    depth = args[0].shape[0]

    def vmem(*shape):
        return pltpu.VMEM(shape, jnp.float32)

    def dma(*shape):
        return pltpu.SemaphoreType.DMA(shape)

    ext = vmem(depth, ROWS, LANES)
    level = vmem(8, depth, ROWS, LANES)
    n0 = 3 * depth + 1
    p0 = (n0 + 15) // 16
    pz = (2 * depth + 15) // 16
    scratch = [ext] * 7 + [vmem(ROWS, LANES), ext]
    scratch += [level, level] + [ext] * 7 + [vmem(depth, *TILE)]
    scratch += [
        vmem(depth, *TILE), vmem(n0, *TILE), vmem(n0, *TILE), vmem(n0, *TILE),
        vmem(2, p0, *TILE), vmem(p0, ROWS, 128), vmem(p0, ROWS, 128),
        vmem(NEWTON, HALO, depth, *TILE), vmem(NEWTON, HALO, depth, *TILE), vmem(NEWTON, HALO, depth, *TILE),
        vmem(NEWTON, HALO, 2, 1, *TILE), vmem(NEWTON, HALO, 1, ROWS, 128), vmem(NEWTON, HALO, 1, ROWS, 128),
        vmem(NEWTON, 2 * depth, *TILE), vmem(NEWTON, 2 * depth, *TILE), vmem(NEWTON, 2 * depth, *TILE),
        vmem(NEWTON, 2, pz, *TILE), vmem(NEWTON, pz, ROWS, 128), vmem(NEWTON, pz, ROWS, 128),
        vmem(NEWTON, 8, *TILE), vmem(NEWTON, 3, gyn, 8, *TILE), vmem(NEWTON, *TILE), vmem(NEWTON, 3, gyn, *TILE),
        vmem(8, ROWS, 128 * gyn), vmem(ROWS, 128), vmem(gyn, ROWS, 128),
        vmem(NEWTON, *TILE), vmem(NEWTON, gyn, *TILE), vmem(NEWTON, gxn, *TILE), vmem(NEWTON, *TILE),
        dma(8), dma(8), dma(NEWTON, HALO, 8), dma(NEWTON, HALO, 8), dma(NEWTON, 8), dma(NEWTON, 8),
        dma(NEWTON, 3, gyn), dma(NEWTON, 3, gyn), dma(NEWTON, 3, gyn), dma(NEWTON, 3, gyn),
        dma(NEWTON, gyn), dma(NEWTON, gyn), dma(NEWTON, gxn), dma(NEWTON, gxn),
    ]
    return pl.pallas_call(
        functools.partial(kernel, gxn, gyn, depth),
        out_shape=jax.ShapeDtypeStruct(args[0].shape, jnp.float32),
        in_specs=[pl.BlockSpec(memory_space=pltpu.VMEM)] * 4 + [pl.BlockSpec(memory_space=pltpu.SMEM)] * 4,
        out_specs=pl.BlockSpec(memory_space=pltpu.VMEM),
        scratch_shapes=scratch,
        compiler_params=pltpu.CompilerParams(
            collective_id=0, has_side_effects=True, vmem_limit_bytes=40 * 1024 * 1024),
    )(*args)


def solution(mesh):
    cells = P(None, "gx", "gy")
    placed = (cells, cells, cells, P("gx", "gy"), P(), P(), P(), P())
    return jax.shard_map(
        functools.partial(on_device, mesh.shape["gx"], mesh.shape["gy"]),
        mesh=mesh, in_specs=placed, out_specs=cells, check_vma=False,
    )
```

```python
import functools

import jax
import jax.numpy as jnp
from jax import lax
from jax.experimental import pallas as pl
from jax.experimental.pallas import tpu as pltpu
from jax.sharding import PartitionSpec as P

NEWTON = 2
COARSE_SWEEPS = 4
OMEGA = 0.8
STORAGE = 0.05
EPSILON = 1e-06

ROWS = 24
LANES = 256
TILE = (8, 128)
MESH = pl.DeviceIdType.MESH
DIRECTIONS = tuple((dx, dy) for dx in (-1, 0, 1) for dy in (-1, 0, 1) if (dx, dy) != (0, 0))
HALO = 5


def roll(field, shift, axis):
    size = field.shape[axis]
    return pltpu.roll(field, shift % size if isinstance(shift, int) else shift, axis)


def iota(shape, axis):
    return lax.broadcasted_iota(jnp.int32, shape, axis)


def pair(field, step, axis):
    low = (iota(field.shape, axis) & step) == 0
    return jnp.where(low, roll(field, -step, axis), roll(field, step, axis))


def sum_pair(field, step, axis):
    return field + pair(field, step, axis)


def sum_four(field, step):
    return sum_pair(sum_pair(field, step, 1), step, 0)


def spread_low(field, step, axis):
    low = (iota(field.shape, axis) & step) == 0
    return jnp.where(low, field, roll(field, step, axis))


def spread_high(field, step, axis):
    low = (iota(field.shape, axis) & step) == 0
    return jnp.where(low, roll(field, -step, axis), field)


def coarsen(coefs, step):
    storage, west, east, south, north, lower, upper = coefs
    return (
        sum_four(storage, step),
        spread_low(sum_pair(west, step, 1), step, 0),
        spread_high(sum_pair(east, step, 1), step, 0),
        spread_low(sum_pair(south, step, 0), step, 1),
        spread_high(sum_pair(north, step, 0), step, 1),
        sum_four(lower, step),
        sum_four(upper, step),
    )


def kernel(
    gxn, gyn, depth,
    pressure, saturation_old, soil_type, recharge, ksat_in, alpha_in, porosity_in, residual_in,
    out,
    old, state, sat, con, alp, por, res, rch, rel,
    lev0, lev1, g, b0, xa, xb, b1, ya, yb, z0,
    soil, ksat, alpha_t, porosity_t, residual_t,
    own, msg0, recv0_w, recv0_e, pack0, recv0_n, recv0_s,
    msg, recv_w, recv_e, pack, recv_n, recv_s,
    coarse_out, coarse_in, rhs_out, rhs_in, strip, strip_sum, solved,
    part_out, part_y, part_x, whole_x,
    local, s0, r0, sh, rh, sc, rc, sb, rb, sy, ry, sx, rx,
):
    gx, gy = lax.axis_index("gx"), lax.axis_index("gy")
    has_w, has_e = gx > 0, gx < gxn - 1
    has_s, has_n = gy > 0, gy < gyn - 1
    last = depth - 1

    def inside(dx, dy):
        x, y = gx + dx, gy + dy
        return (x >= 0) & (x < gxn) & (y >= 0) & (y < gyn)

    def place(dx, dy):
        return (jnp.clip(gx + dx, 0, gxn - 1), jnp.clip(gy + dy, 0, gyn - 1))

    assert depth % 2 == 0
    half = depth // 2
    fetches = [
        pltpu.make_async_copy(src, dst, local.at[i])
        for i, (src, dst) in enumerate((
            (soil_type, soil), (pressure, msg0.at[1, pl.ds(0, depth)]),
            (saturation_old, msg0.at[2, pl.ds(0, depth)]), (recharge, msg0.at[2, depth]),
            (ksat_in, ksat), (alpha_in, alpha_t), (porosity_in, porosity_t), (residual_in, residual_t)))
    ]
    for fetch in fetches:
        fetch.start()

    for ref in (recv0_w, recv0_e, recv0_n, recv0_s, recv_w, recv_e, recv_n, recv_s,
                coarse_in, rhs_in, pack0, pack):
        ref[...] = jnp.zeros(ref.shape, ref.dtype)

    barrier = pltpu.get_barrier_semaphore()
    for dx in (-1, 0, 1):
        for j in range(gyn):
            if (dx, j) != (0, 0):
                @pl.when(inside(dx, 0))
                def _():
                    pl.semaphore_signal(barrier, inc=1, device_id=(jnp.clip(gx + dx, 0, gxn - 1), lax.rem(gy + j, gyn)), device_id_type=MESH)
    for j in range(1, gxn):
        x = lax.rem(gx + j, gxn)
        @pl.when((x != gx - 1) & (x != gx + 1))
        def _():
            pl.semaphore_signal(barrier, inc=1, device_id=(x, gy), device_id_type=MESH)
    strips = 1 + has_w.astype(jnp.int32) + has_e.astype(jnp.int32)

    lane8, row8 = iota(TILE, 1), iota(TILE, 0)
    slot8 = (row8 & 3) * 4 + (lane8 & 3)
    lane_e, row_e = iota((ROWS, LANES), 1), iota((ROWS, LANES), 0)
    lane24 = iota((ROWS, 128), 1)
    even_row = (row_e & 1) == 0

    def put_edges(packs, k, block):
        at = lax.rem(k, 16)
        moved = roll(block, at * 8, 1)
        group = lane8 >> 3
        where = k // 16
        packs[0, where] = jnp.where(group == at, moved, packs[0, where])
        packs[1, where] = jnp.where(group == lax.rem(at + 15, 16), moved, packs[1, where])

    def halo_copies(blocks, packs, to_w, to_e, to_n, to_s, send, recv):
        copies = []
        for d, (dx, dy) in enumerate(DIRECTIONS):
            rows = pl.ds(8 * (1 - dx), 8)
            if dy == 0:
                src, dst = blocks, (to_w if dx > 0 else to_e)
            elif dy > 0:
                src, dst = packs.at[1], to_s.at[:, rows]
            else:
                src, dst = packs.at[0], to_n.at[:, rows]
            copy = pltpu.make_async_remote_copy(
                src_ref=src, dst_ref=dst, send_sem=send.at[d], recv_sem=recv.at[d],
                device_id=place(dx, dy), device_id_type=MESH)
            copies.append((copy, inside(dx, dy), inside(-dx, -dy)))
        return copies

    def gather_copies(src, dst, send, recv):
        copies = []
        for dx in (-1, 0, 1):
            for j in range(gyn):
                if (dx, j) == (0, 0):
                    continue
                copy = pltpu.make_async_remote_copy(
                    src_ref=src, dst_ref=dst.at[1 - dx, gy], send_sem=send.at[1 - dx, j], recv_sem=recv.at[1 - dx, j],
                    device_id=(jnp.clip(gx + dx, 0, gxn - 1), lax.rem(gy + j, gyn)), device_id_type=MESH)
                copies.append((copy, inside(dx, 0), inside(-dx, 0)))
        return copies

    def sum_copies(src, dst, send, recv, count, along_x):
        copies = []
        for j in range(1, count):
            to = (lax.rem(gx + j, gxn), gy) if along_x else (gx, lax.rem(gy + j, gyn))
            copy = pltpu.make_async_remote_copy(
                src_ref=src, dst_ref=dst.at[j], send_sem=send.at[j], recv_sem=recv.at[j],
                device_id=to, device_id_type=MESH)
            copies.append((copy, None, None))
        return copies

    def each(copies, do, which):
        for entry in copies:
            if entry[which] is None:
                do(entry[0])
            else:
                @pl.when(entry[which])
                def _():
                    do(entry[0])

    def start(copies):
        each(copies, lambda copy: copy.start(), 1)

    def arrive(copies):
        each(copies, lambda copy: copy.wait_recv(), 2)

    def sent(copies):
        each(copies, lambda copy: copy.wait_send(), 1)

    def extended(k, block, from_w, from_e, from_n, from_s):
        left = jnp.concatenate([from_w[k], block, from_e[k]], axis=0)
        back = lax.rem(16 - lax.rem(k, 16), 16) * 8
        where = k // 16
        north, south = roll(from_n[where], back, 1), roll(from_s[where], back, 1)
        right = jnp.where(lane24 < 8, north, jnp.where(lane24 >= 120, south, 0.0))
        return jnp.concatenate([left, right], axis=1)

    def layers(body, count=depth):
        def step(k, carry):
            body(k)
            return carry
        lax.fori_loop(0, count, step, 0, unroll=True)

    def first_copies(group, count):
        rows = pl.ds(0, count)
        return halo_copies(msg0.at[group, rows], pack0.at[group], recv0_w.at[group, rows], recv0_e.at[group, rows],
                           recv0_n.at[group], recv0_s.at[group], s0.at[group], r0.at[group])

    def first_ext(group, k):
        return extended(k, msg0[group, k], recv0_w.at[group], recv0_e.at[group], recv0_n.at[group], recv0_s.at[group])

    fetches[0].wait()

    def stage(k):
        msg0[0, k] = soil[k].astype(jnp.float32)
        put_edges(pack0.at[0], k, msg0[0, k])
    layers(stage)
    for fetch in fetches[1:]:
        fetch.wait()
    layers(lambda k: put_edges(pack0.at[1], k, msg0[1, k]))
    layers(lambda k: put_edges(pack0.at[2], k, msg0[2, k]), depth + 1)
    pl.semaphore_wait(barrier, gyn * strips - 1 + gxn - strips)
    groups = [first_copies(0, depth), first_copies(1, depth), first_copies(2, depth + 1)]
    for group in groups:
        start(group)

    valid = (
        ((row_e >= 8) | has_w) & ((row_e < 16) | has_e)
        & ((lane_e < 128) | ((lane_e < 136) & has_n) | ((lane_e >= 248) & has_s))
    )
    arrive(groups[0])

    def look_up(k):
        kinds = first_ext(0, k)
        values = [jnp.zeros((ROWS, LANES), jnp.float32) for _ in range(4)]
        for kind in range(ksat.shape[0]):
            here = kinds == float(kind)
            values = [jnp.where(here, table[kind], value) for table, value in zip((ksat, alpha_t, porosity_t, residual_t), values)]
        con[k] = jnp.where(valid, values[0], 0.0)
        alp[k], por[k], res[k] = values[1], values[2], values[3]
    layers(look_up)
    arrive(groups[1])

    def unpack_pressure(k):
        old[k] = first_ext(1, k)
        state[k] = old[k]
    layers(unpack_pressure)
    arrive(groups[2])

    def unpack_saturation(k):
        sat[k] = first_ext(2, k)
    layers(unpack_saturation)
    rch[...] = first_ext(2, depth)
    for group in groups:
        sent(group)

    def pulled(level, ref, k, field, step):
        total = level[2, k] * roll(field, step, 0) + level[3, k] * roll(field, -step, 0)
        total = total + level[4, k] * roll(field, step, 1) + level[5, k] * roll(field, -step, 1)
        below, above = ref[jnp.maximum(k - 1, 0)], ref[jnp.minimum(k + 1, last)]
        return total + level[6, k] * below + level[7, k] * above

    def residual(level, ref, rhs, k, step):
        field = ref[k]
        return field, rhs[k] - level[0, k] * field + pulled(level, ref, k, field, step)

    def sweep(level, src, rhs, dst, step):
        def body(k):
            field, left = residual(level, src, rhs, k, step)
            dst[k] = field + level[1, k] * left
        layers(body)

    def round_copies(nt, turn, count):
        rows = pl.ds(0, count)
        return halo_copies(msg.at[nt, turn, rows], pack.at[nt, turn], recv_w.at[nt, turn, rows], recv_e.at[nt, turn, rows],
                           recv_n.at[nt, turn], recv_s.at[nt, turn], sh.at[nt, turn], rh.at[nt, turn])

    def round_ext(nt, turn, k):
        return extended(k, msg[nt, turn, k], recv_w.at[nt, turn], recv_e.at[nt, turn],
                        recv_n.at[nt, turn], recv_s.at[nt, turn])

    def precondition(nt, j, rhs, operator):
        def begin(k):
            xa[k] = lev0[1, k] * rhs[k]
        layers(begin)
        sweep(lev0, xa, rhs, xb, 1)

        def down(k):
            _, left = residual(lev0, xb, rhs, k, 1)
            total = sum_four(left, 1)
            b1[k] = total
            ya[k] = lev1[1, k] * total
        layers(down)
        sweep(lev1, ya, b1, yb, 2)
        turn = 2 * j

        def stage_middle(i):
            pair_of = []
            for k in (i, i + half):
                pair_of.append(jnp.where((row8 & 1) == 0, yb[k][8:16, :128], b1[k][8:16, :128]))
            mix = jnp.where((lane8 & 1) == 0, pair_of[0], pair_of[1])
            msg[nt, turn, i] = mix
            put_edges(pack.at[nt, turn], i, mix)
        layers(stage_middle, half)
        halo = round_copies(nt, turn, half)
        start(halo)

        def deep(k, packed):
            _, left = residual(lev1, yb, b1, k, 2)
            return jnp.where(slot8 == k, sum_four(left[8:16, :128], 2), packed)
        packed = lax.fori_loop(0, depth, deep, jnp.zeros(TILE, jnp.float32), unroll=True)
        rhs_out[nt, j] = packed
        rhs_in[nt, j, 1, gy] = packed
        gathers = gather_copies(rhs_out.at[nt, j], rhs_in.at[nt, j], sb.at[nt, j], rb.at[nt, j])
        start(gathers)

        def strips_of(pick):
            return jnp.concatenate(
                [jnp.concatenate([pick(s, y) for y in range(gyn)], axis=1) for s in range(3)], axis=0)

        width = 128 * gyn
        wide_lane, wide_row = iota((ROWS, width), 1), iota((ROWS, width), 0)

        def strip_totals(field):
            total = field[:, :128]
            for y in range(1, gyn):
                total = total + field[:, 128 * y:128 * (y + 1)]
            for step in (4, 8, 16, 32, 64):
                total = total + roll(total, step, 1)
            return sum_pair(total, 4, 0)

        def beneath(e):
            return jnp.where((wide_lane & 3) == 0, roll(roll(e, 1, 0), -3, 1), roll(e, 1, 1))

        def over(e):
            return jnp.where((wide_lane & 3) == 3, roll(roll(e, -1, 0), 3, 1), roll(e, -1, 1))

        if operator is not None:
            arrive(operator)
            diag, south, lower, mixed = (strips_of(lambda s, y: coarse_in[nt, s, y, f]) for f in range(4))
            live = diag > 0.0
            first_row = (wide_row & 4) == 0
            strip[0] = diag
            strip[1] = jnp.where(live, OMEGA / jnp.where(live, diag, 1.0), 0.0)
            strip[2] = jnp.where(first_row, 0.0, roll(mixed, 4, 0))
            strip[3] = jnp.where(first_row, mixed, 0.0)
            strip[4], strip[5] = south, roll(south, -4, 1)
            strip[6], strip[7] = lower, over(lower)
            strip_sum[...] = strip_totals(jnp.where(first_row, 0.0, mixed))
        arrive(gathers)
        b2 = strips_of(lambda s, y: rhs_in[nt, j, s, y])
        below_sum = strip_sum[...]
        some = below_sum > 0.0
        mean = jnp.where(some, strip_totals(b2) / jnp.where(some, below_sum, 1.0), 0.0)

        def coarse_sweep(_, e):
            total = b2 - strip[0] * e
            total = total + strip[2] * roll(e, 4, 0) + strip[3] * roll(e, -4, 0)
            total = total + strip[4] * roll(e, 4, 1) + strip[5] * roll(e, -4, 1)
            total = total + strip[6] * beneath(e) + strip[7] * over(e)
            return e + strip[1] * total
        e2 = lax.fori_loop(0, COARSE_SWEEPS, coarse_sweep, jnp.concatenate([mean] * gyn, axis=1), unroll=True)
        for y in range(gyn):
            solved[y] = e2[:, 128 * y:128 * (y + 1)]
        right = jnp.where(lane24 < 64, solved[jnp.minimum(gy + 1, gyn - 1)], solved[jnp.maximum(gy - 1, 0)])
        around = jnp.concatenate([solved[gy], right], axis=1)
        slot_e = (row_e & 3) * 4 + (lane_e & 3)
        arrive(halo)

        def up(i):
            mix = round_ext(nt, turn, i)
            for k, low in ((i, True), (i + half, False)):
                def put():
                    m = jnp.where(slot_e == k, around, 0.0)
                    m = roll(m, lax.rem(LANES - (k & 3), LANES), 1)
                    m = m + roll(m, 1, 1)
                    m = m + roll(m, 2, 1)
                    m = roll(m, lax.rem(ROWS - (k >> 2), ROWS), 0)
                    m = m + roll(m, 1, 0)
                    m = m + roll(m, 2, 0)
                    both = spread_low(mix, 1, 1) if low else spread_high(mix, 1, 1)
                    ya[k] = m + jnp.where(even_row, both, roll(both, 1, 0))
                    b1[k] = jnp.where(even_row, roll(both, -1, 0), both)
                put()
        layers(up, half)
        sweep(lev1, ya, b1, yb, 2)

        def join(k):
            field, left = residual(lev1, yb, b1, k, 2)
            xb[k] = xb[k] + field + lev1[1, k] * left
        layers(join)
        sweep(lev0, xb, rhs, xa, 1)
        sweep(lev0, xa, rhs, xb, 1)
        sent(gathers)
        sent(halo)

    def applied(k):
        field = xb[k]
        return (lev0[0, k] * field - pulled(lev0, xb, k, field, 1))[8:16, :128]

    def newton(nt, carry):
        def cells(k):
            effective = 1.0 / (1.0 + jnp.exp(-(alp[k] * state[k])))
            saturation = res[k] + (1.0 - res[k]) * effective
            slope = (1.0 - res[k]) * alp[k] * effective * (1.0 - effective)
            rel[k] = effective * effective
            xa[k] = STORAGE + por[k] * slope
            g[k] = por[k] * (saturation - sat[k]) + STORAGE * (state[k] - old[k])
        layers(cells)

        def faces(k):
            def face(con_n, rel_n):
                total = con[k] + con_n
                live = total > 0.0
                return 2.0 * con[k] * con_n / jnp.where(live, total, 1.0) * (0.5 * (rel[k] + rel_n))
            west = face(roll(con[k], 1, 0), roll(rel[k], 1, 0))
            south = face(roll(con[k], 1, 1), roll(rel[k], 1, 1))
            lower = face(con[jnp.maximum(k - 1, 0)], rel[jnp.maximum(k - 1, 0)])
            lev0[2, k], lev0[3, k] = west, roll(west, -1, 0)
            lev0[4, k], lev0[5, k] = south, roll(south, -1, 1)
            lev0[6, k] = jnp.where(k > 0, lower, 0.0)
        layers(faces)

        def operators(k, packed):
            west, east, south, north, lower = (lev0[f, k] for f in range(2, 7))
            upper = jnp.where(k < last, lev0[6, jnp.minimum(k + 1, last)], 0.0)
            lev0[7, k] = upper
            fine = (xa[k], west, east, south, north, lower, upper)
            diag = fine[0] + west + east + south + north + lower + upper
            lev0[0, k], lev0[1, k] = diag, OMEGA / diag
            here = state[k]
            below, above = state[jnp.maximum(k - 1, 0)], state[jnp.minimum(k + 1, last)]
            flux = (
                west * (here - roll(here, 1, 0)) + east * (here - roll(here, -1, 0))
                + south * (here - roll(here, 1, 1)) + north * (here - roll(here, -1, 1))
                + lower * (here - below + 1.0) + upper * (here - above - 1.0)
            )
            g[k] = jnp.where(k == last, rch[...], 0.0) - g[k] - flux
            middle = coarsen(fine, 1)
            diag = middle[0]
            for f in range(1, 7):
                lev1[f + 1, k] = middle[f]
                diag = diag + middle[f]
            lev1[0, k], lev1[1, k] = diag, OMEGA / diag
            coarse = coarsen([field[8:16, :128] for field in middle], 2)
            diag = coarse[0]
            for f in range(1, 7):
                diag = diag + coarse[f]
            mixed = jnp.where((row8 & 4) == 0, coarse[2], sum_pair(coarse[0], 4, 0))
            return tuple(jnp.where(slot8 == k, field, so_far)
                         for field, so_far in zip((diag, coarse[3], coarse[5], mixed), packed))
        packed = lax.fori_loop(0, depth, operators, (jnp.zeros(TILE, jnp.float32),) * 4, unroll=True)
        for f in range(4):
            coarse_out[nt, f] = packed[f]
            coarse_in[nt, 1, gy, f] = packed[f]
        operator = gather_copies(coarse_out.at[nt], coarse_in.at[nt], sc.at[nt], rc.at[nt])
        start(operator)
        precondition(nt, 0, g, operator)

        zeros = jnp.zeros(TILE, jnp.float32)

        def image(k, sums):
            gg, gp, pp = sums
            mine = g[k][8:16, :128]
            diff = applied(k) - mine
            z0[k] = xb[k][8:16, :128]
            msg[nt, 3, k] = z0[k]
            put_edges(pack.at[nt, 3], k, z0[k])
            own[k] = diff
            msg[nt, 1, k] = diff
            put_edges(pack.at[nt, 1], k, diff)
            return gg + mine * mine, gp + mine * diff, pp + diff * diff
        gg, gp, pp = lax.fori_loop(0, depth, image, (zeros, zeros, zeros), unroll=True)
        halo = round_copies(nt, 1, depth)
        halo_z = round_copies(nt, 3, depth)
        halo_u = round_copies(nt, 4, depth)
        start(halo)
        arrive(halo)

        @pl.when(nt < NEWTON - 1)
        def _():
            start(halo_z)

        def spread(k):
            b0[k] = round_ext(nt, 1, k)
        layers(spread)
        sent(halo)
        precondition(nt, 1, b0, None)

        def second(k, sums):
            gs, ps, ss = sums
            mine = g[k][8:16, :128]
            im = applied(k)
            u = xb[k][8:16, :128]
            msg[nt, 4, k] = u
            put_edges(pack.at[nt, 4], k, u)
            return gs + mine * im, ps + own[k] * im, ss + im * im
        gs, ps, ss = lax.fori_loop(0, depth, second, (zeros, zeros, zeros), unroll=True)

        rows = [jnp.sum(item, axis=0, keepdims=True) for item in (gg, gp, pp, gs, ps, ss)]
        tile = zeros
        for i, item in enumerate(rows):
            tile = jnp.where(row8 == i, jnp.broadcast_to(item, TILE), tile)
        part_out[nt] = tile
        along_y = sum_copies(part_out.at[nt], part_y.at[nt], sy.at[nt], ry.at[nt], gyn, False)
        start(along_y)

        @pl.when(nt < NEWTON - 1)
        def _():
            start(halo_u)
        arrive(along_y)
        for j in range(1, gyn):
            tile = tile + part_y[nt, j]
        whole_x[nt] = tile
        along_x = sum_copies(whole_x.at[nt], part_x.at[nt], sx.at[nt], rx.at[nt], gxn, True)
        start(along_x)
        arrive(along_x)
        for j in range(1, gxn):
            tile = tile + part_x[nt, j]
        totals = jnp.broadcast_to(jnp.sum(tile, axis=1, keepdims=True), (8, LANES))
        gg, gp, pp, gs, ps, ss = (totals[i:i + 1] for i in range(6))

        square = gg + EPSILON
        beta = jnp.sqrt(square)
        h00 = (gg + gp) / square
        a = (EPSILON - gp) / square
        vv = jnp.maximum(pp + 2.0 * a * gp + a * a * gg, 0.0)
        h10 = jnp.sqrt(vv / square + EPSILON)
        kappa = 1.0 / (beta * h10)
        gw = gs + a * gp + a * gg
        h01 = kappa / beta * gw
        h11 = kappa * kappa * (ps + a * pp + a * gp + a * gw)
        ww = kappa * kappa * (ss + 2.0 * a * (ps + gs) + a * a * (pp + 2.0 * gp + gg))
        v00 = gg / square
        v11 = kappa * kappa * vv
        v01 = kappa / beta * (gp + a * gg)
        rest = ww - h01 * h01 * (2.0 - v00) - h11 * h11 * (2.0 - v11) + 2.0 * h01 * h11 * v01
        h21_sq = jnp.maximum(rest, 0.0) + EPSILON
        m00 = h00 * h00 + h10 * h10
        m01 = h00 * h01 + h10 * h11
        m11 = h01 * h01 + h11 * h11 + h21_sq
        q0, q1 = beta * h00, beta * h01
        factor = m01 / m00
        y1 = (q1 - factor * q0) / (m11 - factor * m01)
        y0 = (q0 - m01 * y1) / m00
        first_weight = y0 / beta + y1 * kappa * a
        second_weight = y1 * kappa

        @pl.when(nt < NEWTON - 1)
        def _():
            arrive(halo_z)
            arrive(halo_u)

            def advance(k):
                state[k] = state[k] + first_weight * round_ext(nt, 3, k) + second_weight * round_ext(nt, 4, k)
            layers(advance)
            sent(halo_z)
            sent(halo_u)

        @pl.when(nt == NEWTON - 1)
        def _():
            def finish(k):
                out[k] = (state[k][8:16, :128] + first_weight[:, :128] * z0[k]
                          + second_weight[:, :128] * msg[nt, 4, k])
            layers(finish)
        sent(operator)
        sent(along_y)
        sent(along_x)
        return carry

    lax.fori_loop(0, NEWTON, newton, 0)


def on_device(gxn, gyn, *args):
    depth = args[0].shape[0]

    def vmem(*shape):
        return pltpu.VMEM(shape, jnp.float32)

    def dma(*shape):
        return pltpu.SemaphoreType.DMA(shape)

    ext = vmem(depth, ROWS, LANES)
    level = vmem(8, depth, ROWS, LANES)
    n0 = depth + 1
    assert n0 <= 16
    scratch = [ext] * 7 + [vmem(ROWS, LANES), ext]
    scratch += [level, level] + [ext] * 7 + [vmem(depth, *TILE)]
    scratch += [pltpu.VMEM((depth,) + TILE, jnp.int32)] + [pltpu.SMEM(item.shape, jnp.float32) for item in args[4:]]
    scratch += [
        vmem(depth, *TILE), vmem(3, n0, *TILE), vmem(3, n0, *TILE), vmem(3, n0, *TILE),
        vmem(3, 2, 1, *TILE), vmem(3, 1, ROWS, 128), vmem(3, 1, ROWS, 128),
        vmem(NEWTON, HALO, depth, *TILE), vmem(NEWTON, HALO, depth, *TILE), vmem(NEWTON, HALO, depth, *TILE),
        vmem(NEWTON, HALO, 2, 1, *TILE), vmem(NEWTON, HALO, 1, ROWS, 128), vmem(NEWTON, HALO, 1, ROWS, 128),
        vmem(NEWTON, 4, *TILE), vmem(NEWTON, 3, gyn, 4, *TILE), vmem(NEWTON, 2, *TILE), vmem(NEWTON, 2, 3, gyn, *TILE),
        vmem(8, ROWS, 128 * gyn), vmem(ROWS, 128), vmem(gyn, ROWS, 128),
        vmem(NEWTON, *TILE), vmem(NEWTON, gyn, *TILE), vmem(NEWTON, gxn, *TILE), vmem(NEWTON, *TILE),
        dma(8), dma(3, 8), dma(3, 8), dma(NEWTON, HALO, 8), dma(NEWTON, HALO, 8),
        dma(NEWTON, 3, gyn), dma(NEWTON, 3, gyn), dma(NEWTON, 2, 3, gyn), dma(NEWTON, 2, 3, gyn),
        dma(NEWTON, gyn), dma(NEWTON, gyn), dma(NEWTON, gxn), dma(NEWTON, gxn),
    ]
    return pl.pallas_call(
        functools.partial(kernel, gxn, gyn, depth),
        out_shape=jax.ShapeDtypeStruct(args[0].shape, jnp.float32),
        in_specs=[pl.BlockSpec(memory_space=pl.ANY)] * 8,
        out_specs=pl.BlockSpec(memory_space=pltpu.VMEM),
        scratch_shapes=scratch,
        compiler_params=pltpu.CompilerParams(
            collective_id=0, has_side_effects=True, vmem_limit_bytes=40 * 1024 * 1024),
    )(*args)


def solution(mesh):
    cells = P(None, "gx", "gy")
    placed = (cells, cells, cells, P("gx", "gy"), P(), P(), P(), P())
    return jax.shard_map(
        functools.partial(on_device, mesh.shape["gx"], mesh.shape["gy"]),
        mesh=mesh, in_specs=placed, out_specs=cells, check_vma=False,
    )
```

```python
import functools

import jax
import jax.numpy as jnp
from jax import lax
from jax.experimental import pallas as pl
from jax.experimental.pallas import tpu as pltpu
from jax.sharding import PartitionSpec as P

NEWTON = 2
COARSE_SWEEPS = 4
OMEGA = 0.8
STORAGE = 0.05
EPSILON = 1e-06

ROWS = 24
LANES = 256
TILE = (8, 128)
MESH = pl.DeviceIdType.MESH
DIRECTIONS = tuple((dx, dy) for dx in (-1, 0, 1) for dy in (-1, 0, 1) if (dx, dy) != (0, 0))
HALO = 5


def roll(field, shift, axis):
    size = field.shape[axis]
    return pltpu.roll(field, shift % size if isinstance(shift, int) else shift, axis)


def iota(shape, axis):
    return lax.broadcasted_iota(jnp.int32, shape, axis)


def pair(field, step, axis):
    low = (iota(field.shape, axis) & step) == 0
    return jnp.where(low, roll(field, -step, axis), roll(field, step, axis))


def sum_pair(field, step, axis):
    return field + pair(field, step, axis)


def sum_four(field, step):
    return sum_pair(sum_pair(field, step, 1), step, 0)


def spread_low(field, step, axis):
    low = (iota(field.shape, axis) & step) == 0
    return jnp.where(low, field, roll(field, step, axis))


def spread_high(field, step, axis):
    low = (iota(field.shape, axis) & step) == 0
    return jnp.where(low, roll(field, -step, axis), field)


def coarsen(coefs, step):
    storage, west, east, south, north, lower, upper = coefs
    return (
        sum_four(storage, step),
        spread_low(sum_pair(west, step, 1), step, 0),
        spread_high(sum_pair(east, step, 1), step, 0),
        spread_low(sum_pair(south, step, 0), step, 1),
        spread_high(sum_pair(north, step, 0), step, 1),
        sum_four(lower, step),
        sum_four(upper, step),
    )


def kernel(
    gxn, gyn, depth,
    pressure, saturation_old, soil_type, recharge, ksat_in, alpha_in, porosity_in, residual_in,
    out,
    old, state, sat, con, alp, por, res, rch, rel, stored,
    lev0, lev1, g, b0, xa, xb, b1, ya, yb, z0,
    soil, ksat, alpha_t, porosity_t, residual_t,
    own, msg0, recv0_w, recv0_e, pack0, recv0_n, recv0_s,
    msg, recv_w, recv_e, pack, recv_n, recv_s,
    coarse_out, coarse_in, rhs_out, rhs_in, strip, strip_sum, solved,
    part_out, part_y, part_x, whole_x,
    local, s0, r0, sh, rh, sc, rc, sb, rb, sy, ry, sx, rx,
):
    gx, gy = lax.axis_index("gx"), lax.axis_index("gy")
    has_w, has_e = gx > 0, gx < gxn - 1
    has_s, has_n = gy > 0, gy < gyn - 1
    last = depth - 1

    def inside(dx, dy):
        x, y = gx + dx, gy + dy
        return (x >= 0) & (x < gxn) & (y >= 0) & (y < gyn)

    def place(dx, dy):
        return (jnp.clip(gx + dx, 0, gxn - 1), jnp.clip(gy + dy, 0, gyn - 1))

    assert depth % 2 == 0
    half = depth // 2
    fetches = [
        pltpu.make_async_copy(src, dst, local.at[i])
        for i, (src, dst) in enumerate((
            (soil_type, soil), (pressure, msg0.at[1, pl.ds(0, depth)]),
            (saturation_old, msg0.at[2, pl.ds(0, depth)]), (recharge, msg0.at[2, depth]),
            (ksat_in, ksat), (alpha_in, alpha_t), (porosity_in, porosity_t), (residual_in, residual_t)))
    ]
    for fetch in fetches:
        fetch.start()

    for ref in (xa, xb, ya, yb):
        for h in range(2):
            ref[h, pl.ds(0, 8)] = jnp.zeros(TILE, jnp.float32)
            ref[h, pl.ds(8 + ROWS * depth, 8)] = jnp.zeros(TILE, jnp.float32)
    for ref in (recv0_w, recv0_e, recv0_n, recv0_s, recv_w, recv_e, recv_n, recv_s,
                coarse_in, rhs_in, pack0, pack):
        ref[...] = jnp.zeros(ref.shape, ref.dtype)

    barrier = pltpu.get_barrier_semaphore()
    for dx in (-1, 0, 1):
        for j in range(gyn):
            if (dx, j) != (0, 0):
                @pl.when(inside(dx, 0))
                def _():
                    pl.semaphore_signal(barrier, inc=1, device_id=(jnp.clip(gx + dx, 0, gxn - 1), lax.rem(gy + j, gyn)), device_id_type=MESH)
    for j in range(1, gxn):
        x = lax.rem(gx + j, gxn)
        @pl.when((x != gx - 1) & (x != gx + 1))
        def _():
            pl.semaphore_signal(barrier, inc=1, device_id=(x, gy), device_id_type=MESH)
    strips = 1 + has_w.astype(jnp.int32) + has_e.astype(jnp.int32)

    lane8, row8 = iota(TILE, 1), iota(TILE, 0)
    slot8 = (row8 & 3) * 4 + (lane8 & 3)
    lane_e, row_e = iota((ROWS, LANES), 1), iota((ROWS, LANES), 0)
    lane24 = iota((ROWS, 128), 1)
    even_row = (row_e & 1) == 0

    def put_edges(packs, k, block):
        at = (k % 16)
        moved = roll(block, at * 8, 1)
        group = lane8 >> 3
        where = k // 16
        packs[0, where] = jnp.where(group == at, moved, packs[0, where])
        packs[1, where] = jnp.where(group == ((at + 15) % 16), moved, packs[1, where])

    def halo_copies(blocks, packs, to_w, to_e, to_n, to_s, send, recv):
        copies = []
        for d, (dx, dy) in enumerate(DIRECTIONS):
            rows = pl.ds(8 * (1 - dx), 8)
            if dy == 0:
                src, dst = blocks, (to_w if dx > 0 else to_e)
            elif dy > 0:
                src, dst = packs.at[1], to_s.at[:, rows]
            else:
                src, dst = packs.at[0], to_n.at[:, rows]
            copy = pltpu.make_async_remote_copy(
                src_ref=src, dst_ref=dst, send_sem=send.at[d], recv_sem=recv.at[d],
                device_id=place(dx, dy), device_id_type=MESH)
            copies.append((copy, inside(dx, dy), inside(-dx, -dy)))
        return copies

    def gather_copies(src, dst, send, recv):
        copies = []
        for dx in (-1, 0, 1):
            for j in range(gyn):
                if (dx, j) == (0, 0):
                    continue
                copy = pltpu.make_async_remote_copy(
                    src_ref=src, dst_ref=dst.at[1 - dx, gy], send_sem=send.at[1 - dx, j], recv_sem=recv.at[1 - dx, j],
                    device_id=(jnp.clip(gx + dx, 0, gxn - 1), lax.rem(gy + j, gyn)), device_id_type=MESH)
                copies.append((copy, inside(dx, 0), inside(-dx, 0)))
        return copies

    def sum_copies(src, dst, send, recv, count, along_x):
        copies = []
        for j in range(1, count):
            to = (lax.rem(gx + j, gxn), gy) if along_x else (gx, lax.rem(gy + j, gyn))
            copy = pltpu.make_async_remote_copy(
                src_ref=src, dst_ref=dst.at[j], send_sem=send.at[j], recv_sem=recv.at[j],
                device_id=to, device_id_type=MESH)
            copies.append((copy, None, None))
        return copies

    def each(copies, do, which):
        for entry in copies:
            if entry[which] is None:
                do(entry[0])
            else:
                @pl.when(entry[which])
                def _():
                    do(entry[0])

    def start(copies):
        each(copies, lambda copy: copy.start(), 1)

    def arrive(copies):
        each(copies, lambda copy: copy.wait_recv(), 2)

    def sent(copies):
        each(copies, lambda copy: copy.wait_send(), 1)

    def extended(k, block, from_w, from_e, from_n, from_s):
        left = jnp.concatenate([from_w[k], block, from_e[k]], axis=0)
        back = (16 - (k % 16)) % 16 * 8
        where = k // 16
        north, south = roll(from_n[where], back, 1), roll(from_s[where], back, 1)
        right = jnp.where(lane24 < 8, north, jnp.where(lane24 >= 120, south, 0.0))
        return jnp.concatenate([left, right], axis=1)

    def layers(body, count=depth):
        for k in range(count):
            body(k)

    def gather_layers(body, carry):
        for k in range(depth):
            carry = body(k, carry)
        return carry

    def get(ref, k, low=0, count=ROWS, shift=0):
        rows = pl.ds(8 + ROWS * k + low + shift, count)
        return jnp.concatenate([ref[0, rows], ref[1, rows]], axis=1)

    def put(ref, k, field, low=0):
        rows = pl.ds(8 + ROWS * k + low, field.shape[0])
        ref[0, rows] = field[:, :128]
        ref[1, rows] = field[:, 128:]

    def mine_of(ref, k):
        return ref[0, pl.ds(8 + ROWS * k + 8, 8)]

    def below_of(k):
        return max(k - 1, 0)

    def above_of(k):
        return min(k + 1, last)

    def first_copies(group, count):
        rows = pl.ds(0, count)
        return halo_copies(msg0.at[group, rows], pack0.at[group], recv0_w.at[group, rows], recv0_e.at[group, rows],
                           recv0_n.at[group], recv0_s.at[group], s0.at[group], r0.at[group])

    def first_ext(group, k):
        return extended(k, msg0[group, k], recv0_w.at[group], recv0_e.at[group], recv0_n.at[group], recv0_s.at[group])

    fetches[0].wait()

    def stage(k):
        msg0[0, k] = soil[k].astype(jnp.float32)
        put_edges(pack0.at[0], k, msg0[0, k])
    layers(stage)
    for fetch in fetches[1:]:
        fetch.wait()
    layers(lambda k: put_edges(pack0.at[1], k, msg0[1, k]))
    layers(lambda k: put_edges(pack0.at[2], k, msg0[2, k]), depth + 1)
    pl.semaphore_wait(barrier, gyn * strips - 1 + gxn - strips)
    groups = [first_copies(0, depth), first_copies(1, depth), first_copies(2, depth + 1)]
    for group in groups:
        start(group)

    valid = (
        ((row_e >= 8) | has_w) & ((row_e < 16) | has_e)
        & ((lane_e < 128) | ((lane_e < 136) & has_n) | ((lane_e >= 248) & has_s))
    )
    arrive(groups[0])

    def look_up(k):
        kinds = first_ext(0, k)
        values = [jnp.zeros((ROWS, LANES), jnp.float32) for _ in range(4)]
        for kind in range(ksat.shape[0]):
            here = kinds == float(kind)
            values = [jnp.where(here, table[kind], value) for table, value in zip((ksat, alpha_t, porosity_t, residual_t), values)]
        con[k] = jnp.where(valid, values[0], 0.0)
        alp[k], por[k], res[k] = values[1], values[2], values[3]
    layers(look_up)
    arrive(groups[1])

    def unpack_pressure(k):
        old[k] = first_ext(1, k)
        state[k] = old[k]
    layers(unpack_pressure)
    arrive(groups[2])

    def unpack_saturation(k):
        sat[k] = first_ext(2, k)
    layers(unpack_saturation)
    rch[...] = first_ext(2, depth)
    for group in groups:
        sent(group)

    def pulled(level, ref, k, field, step, low, count):
        faces = [get(level.at[f], k, low, count) for f in range(2, 8)]
        total = faces[0] * get(ref, k, low, count, -step) + faces[1] * get(ref, k, low, count, step)
        total = total + faces[2] * roll(field, step, 1) + faces[3] * roll(field, -step, 1)
        total = total + faces[4] * get(ref, below_of(k), low, count)
        return total + faces[5] * get(ref, above_of(k), low, count)

    def residual(level, ref, rhs, k, step, low=0, count=ROWS):
        field = get(ref, k, low, count)
        around = pulled(level, ref, k, field, step, low, count)
        return field, get(rhs, k, low, count) - get(level.at[0], k, low, count) * field + around

    def sweep(level, src, rhs, dst, step, low=0, count=ROWS):
        def body(k):
            field, left = residual(level, src, rhs, k, step, low, count)
            put(dst, k, field + get(level.at[1], k, low, count) * left, low)
        layers(body)

    def round_copies(nt, turn, count):
        rows = pl.ds(0, count)
        return halo_copies(msg.at[nt, turn, rows], pack.at[nt, turn], recv_w.at[nt, turn, rows], recv_e.at[nt, turn, rows],
                           recv_n.at[nt, turn], recv_s.at[nt, turn], sh.at[nt, turn], rh.at[nt, turn])

    def round_ext(nt, turn, k):
        return extended(k, msg[nt, turn, k], recv_w.at[nt, turn], recv_e.at[nt, turn],
                        recv_n.at[nt, turn], recv_s.at[nt, turn])

    def precondition(nt, j, rhs, operator):
        def begin(k):
            put(xa, k, get(lev0.at[1], k) * get(rhs, k))
        layers(begin)
        sweep(lev0, xa, rhs, xb, 1)

        def down(k):
            _, left = residual(lev0, xb, rhs, k, 1, 4, 16)
            total = sum_four(left, 1)
            put(b1, k, total, 4)
            put(ya, k, get(lev1.at[1], k, 4, 16) * total, 4)
        layers(down)
        sweep(lev1, ya, b1, yb, 2, 4, 16)
        turn = 2 * j

        def stage_middle(i):
            pair_of = []
            for k in (i, i + half):
                pair_of.append(jnp.where((row8 & 1) == 0, mine_of(yb, k), mine_of(b1, k)))
            mix = jnp.where((lane8 & 1) == 0, pair_of[0], pair_of[1])
            msg[nt, turn, i] = mix
            put_edges(pack.at[nt, turn], i, mix)
        layers(stage_middle, half)
        halo = round_copies(nt, turn, half)
        start(halo)

        def deep(k, packed):
            _, left = residual(lev1, yb, b1, k, 2, 8, 8)
            return jnp.where(slot8 == k, sum_four(left[:, :128], 2), packed)
        packed = gather_layers(deep, jnp.zeros(TILE, jnp.float32))
        rhs_out[nt, j] = packed
        rhs_in[nt, j, 1, gy] = packed
        gathers = gather_copies(rhs_out.at[nt, j], rhs_in.at[nt, j], sb.at[nt, j], rb.at[nt, j])
        start(gathers)

        def strips_of(pick):
            return jnp.concatenate(
                [jnp.concatenate([pick(s, y) for y in range(gyn)], axis=1) for s in range(3)], axis=0)

        width = 128 * gyn
        wide_lane, wide_row = iota((ROWS, width), 1), iota((ROWS, width), 0)

        def strip_totals(field):
            total = field[:, :128]
            for y in range(1, gyn):
                total = total + field[:, 128 * y:128 * (y + 1)]
            for step in (4, 8, 16, 32, 64):
                total = total + roll(total, step, 1)
            return sum_pair(total, 4, 0)

        def beneath(e):
            return jnp.where((wide_lane & 3) == 0, roll(roll(e, 1, 0), -3, 1), roll(e, 1, 1))

        def over(e):
            return jnp.where((wide_lane & 3) == 3, roll(roll(e, -1, 0), 3, 1), roll(e, -1, 1))

        if operator is not None:
            arrive(operator)
            diag, south, lower, mixed = (strips_of(lambda s, y: coarse_in[nt, s, y, f]) for f in range(4))
            live = diag > 0.0
            first_row = (wide_row & 4) == 0
            strip[0] = diag
            strip[1] = jnp.where(live, OMEGA / jnp.where(live, diag, 1.0), 0.0)
            strip[2] = jnp.where(first_row, 0.0, roll(mixed, 4, 0))
            strip[3] = jnp.where(first_row, mixed, 0.0)
            strip[4], strip[5] = south, roll(south, -4, 1)
            strip[6], strip[7] = lower, over(lower)
            strip_sum[...] = strip_totals(jnp.where(first_row, 0.0, mixed))
        arrive(gathers)
        b2 = strips_of(lambda s, y: rhs_in[nt, j, s, y])
        below_sum = strip_sum[...]
        some = below_sum > 0.0
        mean = jnp.where(some, strip_totals(b2) / jnp.where(some, below_sum, 1.0), 0.0)

        def coarse_sweep(_, e):
            total = b2 - strip[0] * e
            total = total + strip[2] * roll(e, 4, 0) + strip[3] * roll(e, -4, 0)
            total = total + strip[4] * roll(e, 4, 1) + strip[5] * roll(e, -4, 1)
            total = total + strip[6] * beneath(e) + strip[7] * over(e)
            return e + strip[1] * total
        e2 = lax.fori_loop(0, COARSE_SWEEPS, coarse_sweep, jnp.concatenate([mean] * gyn, axis=1), unroll=True)
        for y in range(gyn):
            solved[y] = e2[:, 128 * y:128 * (y + 1)]
        right = jnp.where(lane24 < 64, solved[jnp.minimum(gy + 1, gyn - 1)], solved[jnp.maximum(gy - 1, 0)])
        around = jnp.concatenate([solved[gy], right], axis=1)
        slot_e = (row_e & 3) * 4 + (lane_e & 3)
        arrive(halo)

        def up(i):
            mix = round_ext(nt, turn, i)
            for k, low in ((i, True), (i + half, False)):
                def place_layer():
                    m = jnp.where(slot_e == k, around, 0.0)
                    m = roll(m, -(k & 3), 1)
                    m = m + roll(m, 1, 1)
                    m = m + roll(m, 2, 1)
                    m = roll(m, -(k >> 2), 0)
                    m = m + roll(m, 1, 0)
                    m = m + roll(m, 2, 0)
                    both = spread_low(mix, 1, 1) if low else spread_high(mix, 1, 1)
                    put(ya, k, m + jnp.where(even_row, both, roll(both, 1, 0)))
                    put(b1, k, jnp.where(even_row, roll(both, -1, 0), both))
                place_layer()
        layers(up, half)
        sweep(lev1, ya, b1, yb, 2)

        def join(k):
            field, left = residual(lev1, yb, b1, k, 2, 4, 16)
            put(xb, k, get(xb, k, 4, 16) + field + get(lev1.at[1], k, 4, 16) * left, 4)
        layers(join)
        sweep(lev0, xb, rhs, xa, 1, 4, 16)
        sweep(lev0, xa, rhs, xb, 1, 4, 16)
        sent(gathers)
        sent(halo)

    def applied(k):
        field = get(xb, k, 8, 8)
        return (get(lev0.at[0], k, 8, 8) * field - pulled(lev0, xb, k, field, 1, 8, 8))[:, :128]

    def newton(nt, carry):
        def cells(k):
            effective = 1.0 / (1.0 + jnp.exp(-(alp[k] * state[k])))
            saturation = res[k] + (1.0 - res[k]) * effective
            slope = (1.0 - res[k]) * alp[k] * effective * (1.0 - effective)
            rel[k] = effective * effective
            stored[k] = STORAGE + por[k] * slope
            put(g, k, por[k] * (saturation - sat[k]) + STORAGE * (state[k] - old[k]))
        layers(cells)

        def faces(k):
            def face(con_n, rel_n):
                total = con[k] + con_n
                live = total > 0.0
                return 2.0 * con[k] * con_n / jnp.where(live, total, 1.0) * (0.5 * (rel[k] + rel_n))
            west = face(roll(con[k], 1, 0), roll(rel[k], 1, 0))
            south = face(roll(con[k], 1, 1), roll(rel[k], 1, 1))
            lower = face(con[k - 1], rel[k - 1]) if k else jnp.zeros((ROWS, LANES), jnp.float32)
            for f, field in enumerate((west, roll(west, -1, 0), south, roll(south, -1, 1), lower)):
                put(lev0.at[f + 2], k, field)
        layers(faces)

        def operators(k, carried):
            middle_lower, packed = carried
            west, east, south, north, lower = (get(lev0.at[f], k) for f in range(2, 7))
            upper = get(lev0.at[6], k + 1) if k < last else jnp.zeros((ROWS, LANES), jnp.float32)
            put(lev0.at[7], k, upper)
            diag = stored[k] + west + east + south + north + lower + upper
            put(lev0.at[0], k, diag)
            put(lev0.at[1], k, OMEGA / diag)
            here = state[k]
            below, above = state[below_of(k)], state[above_of(k)]
            flux = (
                west * (here - roll(here, 1, 0)) + east * (here - roll(here, -1, 0))
                + south * (here - roll(here, 1, 1)) + north * (here - roll(here, -1, 1))
                + lower * (here - below + 1.0) + upper * (here - above - 1.0)
            )
            gain = rch[...] - get(g, k) if k == last else -get(g, k)
            put(g, k, gain - flux)
            middle_west = spread_low(sum_pair(west, 1, 1), 1, 0)
            middle_south = spread_low(sum_pair(south, 1, 0), 1, 1)
            middle_upper = sum_four(upper, 1)
            middle = (sum_four(stored[k], 1), middle_west, roll(middle_west, -2, 0), middle_south,
                      roll(middle_south, -2, 1), middle_lower, middle_upper)
            diag = middle[0]
            for f in range(1, 7):
                put(lev1.at[f + 1], k, middle[f])
                diag = diag + middle[f]
            put(lev1.at[0], k, diag)
            put(lev1.at[1], k, OMEGA / diag)
            coarse = coarsen([field[8:16, :128] for field in middle], 2)
            diag = coarse[0]
            for f in range(1, 7):
                diag = diag + coarse[f]
            mixed = jnp.where((row8 & 4) == 0, coarse[2], sum_pair(coarse[0], 4, 0))
            return middle_upper, tuple(jnp.where(slot8 == k, field, so_far)
                                       for field, so_far in zip((diag, coarse[3], coarse[5], mixed), packed))
        _, packed = gather_layers(operators, (jnp.zeros((ROWS, LANES), jnp.float32), (jnp.zeros(TILE, jnp.float32),) * 4))
        for f in range(4):
            coarse_out[nt, f] = packed[f]
            coarse_in[nt, 1, gy, f] = packed[f]
        operator = gather_copies(coarse_out.at[nt], coarse_in.at[nt], sc.at[nt], rc.at[nt])
        start(operator)
        precondition(nt, 0, g, operator)

        zeros = jnp.zeros(TILE, jnp.float32)

        def image(k, sums):
            gg, gp, pp = sums
            mine = mine_of(g, k)
            diff = applied(k) - mine
            z0[k] = mine_of(xb, k)
            msg[nt, 3, k] = z0[k]
            put_edges(pack.at[nt, 3], k, z0[k])
            own[k] = diff
            msg[nt, 1, k] = diff
            put_edges(pack.at[nt, 1], k, diff)
            return gg + mine * mine, gp + mine * diff, pp + diff * diff
        gg, gp, pp = gather_layers(image, (zeros, zeros, zeros))
        halo = round_copies(nt, 1, depth)
        halo_z = round_copies(nt, 3, depth)
        halo_u = round_copies(nt, 4, depth)
        start(halo)
        arrive(halo)

        @pl.when(nt < NEWTON - 1)
        def _():
            start(halo_z)

        def spread(k):
            put(b0, k, round_ext(nt, 1, k))
        layers(spread)
        sent(halo)
        precondition(nt, 1, b0, None)

        def second(k, sums):
            gs, ps, ss = sums
            mine = mine_of(g, k)
            im = applied(k)
            u = mine_of(xb, k)
            msg[nt, 4, k] = u
            put_edges(pack.at[nt, 4], k, u)
            return gs + mine * im, ps + own[k] * im, ss + im * im
        gs, ps, ss = gather_layers(second, (zeros, zeros, zeros))

        rows = [jnp.sum(item, axis=0, keepdims=True) for item in (gg, gp, pp, gs, ps, ss)]
        tile = zeros
        for i, item in enumerate(rows):
            tile = jnp.where(row8 == i, jnp.broadcast_to(item, TILE), tile)
        part_out[nt] = tile
        along_y = sum_copies(part_out.at[nt], part_y.at[nt], sy.at[nt], ry.at[nt], gyn, False)
        start(along_y)

        @pl.when(nt < NEWTON - 1)
        def _():
            start(halo_u)
        arrive(along_y)
        for j in range(1, gyn):
            tile = tile + part_y[nt, j]
        whole_x[nt] = tile
        along_x = sum_copies(whole_x.at[nt], part_x.at[nt], sx.at[nt], rx.at[nt], gxn, True)
        start(along_x)
        arrive(along_x)
        for j in range(1, gxn):
            tile = tile + part_x[nt, j]
        totals = jnp.broadcast_to(jnp.sum(tile, axis=1, keepdims=True), (8, LANES))
        gg, gp, pp, gs, ps, ss = (totals[i:i + 1] for i in range(6))

        square = gg + EPSILON
        beta = jnp.sqrt(square)
        h00 = (gg + gp) / square
        a = (EPSILON - gp) / square
        vv = jnp.maximum(pp + 2.0 * a * gp + a * a * gg, 0.0)
        h10 = jnp.sqrt(vv / square + EPSILON)
        kappa = 1.0 / (beta * h10)
        gw = gs + a * gp + a * gg
        h01 = kappa / beta * gw
        h11 = kappa * kappa * (ps + a * pp + a * gp + a * gw)
        ww = kappa * kappa * (ss + 2.0 * a * (ps + gs) + a * a * (pp + 2.0 * gp + gg))
        v00 = gg / square
        v11 = kappa * kappa * vv
        v01 = kappa / beta * (gp + a * gg)
        rest = ww - h01 * h01 * (2.0 - v00) - h11 * h11 * (2.0 - v11) + 2.0 * h01 * h11 * v01
        h21_sq = jnp.maximum(rest, 0.0) + EPSILON
        m00 = h00 * h00 + h10 * h10
        m01 = h00 * h01 + h10 * h11
        m11 = h01 * h01 + h11 * h11 + h21_sq
        q0, q1 = beta * h00, beta * h01
        factor = m01 / m00
        y1 = (q1 - factor * q0) / (m11 - factor * m01)
        y0 = (q0 - m01 * y1) / m00
        first_weight = y0 / beta + y1 * kappa * a
        second_weight = y1 * kappa

        @pl.when(nt < NEWTON - 1)
        def _():
            arrive(halo_z)
            arrive(halo_u)

            def advance(k):
                state[k] = state[k] + first_weight * round_ext(nt, 3, k) + second_weight * round_ext(nt, 4, k)
            layers(advance)
            sent(halo_z)
            sent(halo_u)

        @pl.when(nt == NEWTON - 1)
        def _():
            def finish(k):
                out[k] = (state[k][8:16, :128] + first_weight[:, :128] * z0[k]
                          + second_weight[:, :128] * msg[nt, 4, k])
            layers(finish)
        sent(operator)
        sent(along_y)
        sent(along_x)
        return carry

    lax.fori_loop(0, NEWTON, newton, 0)


def on_device(gxn, gyn, *args):
    depth = args[0].shape[0]

    def vmem(*shape):
        return pltpu.VMEM(shape, jnp.float32)

    def dma(*shape):
        return pltpu.SemaphoreType.DMA(shape)

    ext = vmem(depth, ROWS, LANES)
    flat = ROWS * depth + 16
    level = vmem(8, 2, flat, 128)
    n0 = depth + 1
    assert n0 <= 16
    scratch = [ext] * 7 + [vmem(ROWS, LANES), ext, ext]
    scratch += [level, level] + [vmem(2, flat, 128)] * 7 + [vmem(depth, *TILE)]
    scratch += [pltpu.VMEM((depth,) + TILE, jnp.int32)] + [pltpu.SMEM(item.shape, jnp.float32) for item in args[4:]]
    scratch += [
        vmem(depth, *TILE), vmem(3, n0, *TILE), vmem(3, n0, *TILE), vmem(3, n0, *TILE),
        vmem(3, 2, 1, *TILE), vmem(3, 1, ROWS, 128), vmem(3, 1, ROWS, 128),
        vmem(NEWTON, HALO, depth, *TILE), vmem(NEWTON, HALO, depth, *TILE), vmem(NEWTON, HALO, depth, *TILE),
        vmem(NEWTON, HALO, 2, 1, *TILE), vmem(NEWTON, HALO, 1, ROWS, 128), vmem(NEWTON, HALO, 1, ROWS, 128),
        vmem(NEWTON, 4, *TILE), vmem(NEWTON, 3, gyn, 4, *TILE), vmem(NEWTON, 2, *TILE), vmem(NEWTON, 2, 3, gyn, *TILE),
        vmem(8, ROWS, 128 * gyn), vmem(ROWS, 128), vmem(gyn, ROWS, 128),
        vmem(NEWTON, *TILE), vmem(NEWTON, gyn, *TILE), vmem(NEWTON, gxn, *TILE), vmem(NEWTON, *TILE),
        dma(8), dma(3, 8), dma(3, 8), dma(NEWTON, HALO, 8), dma(NEWTON, HALO, 8),
        dma(NEWTON, 3, gyn), dma(NEWTON, 3, gyn), dma(NEWTON, 2, 3, gyn), dma(NEWTON, 2, 3, gyn),
        dma(NEWTON, gyn), dma(NEWTON, gyn), dma(NEWTON, gxn), dma(NEWTON, gxn),
    ]
    return pl.pallas_call(
        functools.partial(kernel, gxn, gyn, depth),
        out_shape=jax.ShapeDtypeStruct(args[0].shape, jnp.float32),
        in_specs=[pl.BlockSpec(memory_space=pltpu.HBM)] * 8,
        out_specs=pl.BlockSpec(memory_space=pltpu.VMEM),
        scratch_shapes=scratch,
        compiler_params=pltpu.CompilerParams(
            collective_id=0, has_side_effects=True, vmem_limit_bytes=64 * 1024 * 1024),
    )(*args)


def solution(mesh):
    cells = P(None, "gx", "gy")
    placed = (cells, cells, cells, P("gx", "gy"), P(), P(), P(), P())
    return jax.shard_map(
        functools.partial(on_device, mesh.shape["gx"], mesh.shape["gy"]),
        mesh=mesh, in_specs=placed, out_specs=cells, check_vma=False,
    )
```

```python
import functools

import jax
import jax.numpy as jnp
from jax import lax
from jax.experimental import pallas as pl
from jax.experimental.pallas import tpu as pltpu
from jax.sharding import PartitionSpec as P

NEWTON = 2
COARSE_SWEEPS = 4
OMEGA = 0.8
STORAGE = 0.05
EPSILON = 1e-06

ROWS = 24
LANES = 256
TILE = (8, 128)
MESH = pl.DeviceIdType.MESH
DIRECTIONS = tuple((dx, dy) for dx in (-1, 0, 1) for dy in (-1, 0, 1) if (dx, dy) != (0, 0))
HALO = 5


def roll(field, shift, axis):
    size = field.shape[axis]
    return pltpu.roll(field, shift % size if isinstance(shift, int) else shift, axis)


def iota(shape, axis):
    return lax.broadcasted_iota(jnp.int32, shape, axis)


def pair(field, step, axis):
    low = (iota(field.shape, axis) & step) == 0
    return jnp.where(low, roll(field, -step, axis), roll(field, step, axis))


def sum_pair(field, step, axis):
    return field + pair(field, step, axis)


def sum_four(field, step):
    return sum_pair(sum_pair(field, step, 1), step, 0)


def spread_low(field, step, axis):
    low = (iota(field.shape, axis) & step) == 0
    return jnp.where(low, field, roll(field, step, axis))


def spread_high(field, step, axis):
    low = (iota(field.shape, axis) & step) == 0
    return jnp.where(low, roll(field, -step, axis), field)


def coarsen(coefs, step):
    storage, west, east, south, north, lower, upper = coefs
    return (
        sum_four(storage, step),
        spread_low(sum_pair(west, step, 1), step, 0),
        spread_high(sum_pair(east, step, 1), step, 0),
        spread_low(sum_pair(south, step, 0), step, 1),
        spread_high(sum_pair(north, step, 0), step, 1),
        sum_four(lower, step),
        sum_four(upper, step),
    )


def kernel(
    gxn, gyn, depth,
    pressure, saturation_old, soil_type, recharge, ksat_in, alpha_in, porosity_in, residual_in,
    out,
    old, state, sat, con, alp, por, res, rch, rel, stored,
    lev0, lev1, g, b0, xa, xb, b1, ya, yb, z0,
    soil, ksat, alpha_t, porosity_t, residual_t,
    own, msg0, recv0_w, recv0_e, pack0, recv0_n, recv0_s,
    msg, recv_w, recv_e, pack, recv_n, recv_s,
    coarse_out, coarse_in, rhs_out, rhs_in, strip, strip_sum, solved,
    part_out, part_y, part_x, whole_x,
    local, s0, r0, sh, rh, sc, rc, sb, rb, sy, ry, sx, rx,
):
    gx, gy = lax.axis_index("gx"), lax.axis_index("gy")
    has_w, has_e = gx > 0, gx < gxn - 1
    has_s, has_n = gy > 0, gy < gyn - 1
    last = depth - 1

    def place(dx, j):
        return (jnp.clip(gx + dx, 0, gxn - 1), lax.rem(gy + j, gyn))

    assert depth % 2 == 0 and gyn > 2
    half = depth // 2
    fetches = [
        pltpu.make_async_copy(src, dst, local.at[i])
        for i, (src, dst) in enumerate((
            (soil_type, soil), (pressure, msg0.at[1, pl.ds(0, depth)]),
            (saturation_old, msg0.at[2, pl.ds(0, depth)]), (recharge, msg0.at[2, depth]),
            (ksat_in, ksat), (alpha_in, alpha_t), (porosity_in, porosity_t), (residual_in, residual_t)))
    ]
    for fetch in fetches:
        fetch.start()

    for ref in (xa, xb, ya, yb):
        for h in range(2):
            ref[h, pl.ds(0, 8)] = jnp.zeros(TILE, jnp.float32)
            ref[h, pl.ds(8 + ROWS * depth, 8)] = jnp.zeros(TILE, jnp.float32)
    for ref in (recv0_w, recv0_e, recv0_n, recv0_s, recv_w, recv_e, recv_n, recv_s,
                coarse_in, rhs_in, pack0, pack):
        ref[...] = jnp.zeros(ref.shape, ref.dtype)

    barrier = pltpu.get_barrier_semaphore()
    for dx in (-1, 0, 1):
        for j in range(gyn):
            if (dx, j) != (0, 0):
                @pl.when((gx + dx >= 0) & (gx + dx < gxn))
                def _():
                    pl.semaphore_signal(barrier, inc=1, device_id=(jnp.clip(gx + dx, 0, gxn - 1), lax.rem(gy + j, gyn)), device_id_type=MESH)
    for j in range(1, gxn):
        x = lax.rem(gx + j, gxn)
        @pl.when((x != gx - 1) & (x != gx + 1))
        def _():
            pl.semaphore_signal(barrier, inc=1, device_id=(x, gy), device_id_type=MESH)
    strips = 1 + has_w.astype(jnp.int32) + has_e.astype(jnp.int32)

    lane8, row8 = iota(TILE, 1), iota(TILE, 0)
    slot8 = (row8 & 3) * 4 + (lane8 & 3)
    lane_e, row_e = iota((ROWS, LANES), 1), iota((ROWS, LANES), 0)
    lane24 = iota((ROWS, 128), 1)
    even_row = (row_e & 1) == 0

    def put_edges(packs, k, block):
        at = (k % 16)
        moved = roll(block, at * 8, 1)
        group = lane8 >> 3
        where = k // 16
        packs[0, where] = jnp.where(group == at, moved, packs[0, where])
        packs[1, where] = jnp.where(group == ((at + 15) % 16), moved, packs[1, where])

    def halo_copies(blocks, packs, to_w, to_e, to_n, to_s, send, recv, only_x=False):
        copies = []
        for d, (dx, dy) in enumerate(DIRECTIONS):
            rows = pl.ds(8 * (1 - dx), 8)
            if only_x and dy != 0:
                continue
            if dy == 0:
                src, dst = blocks, (to_w if dx > 0 else to_e)
            elif dy > 0:
                src, dst = packs.at[1], to_s.at[:, rows]
            else:
                src, dst = packs.at[0], to_n.at[:, rows]
            copy = pltpu.make_async_remote_copy(
                src_ref=src, dst_ref=dst, send_sem=send.at[d], recv_sem=recv.at[d],
                device_id=place(dx, dy % gyn), device_id_type=MESH)
            copies.append((copy, dx))
        return copies

    def gather_copies(src, dst, send, recv, tiles_for=None):
        copies = []
        for dx in (-1, 0, 1):
            for j in range(gyn):
                if (dx, j) == (0, 0):
                    continue
                tiles = pl.ds(*tiles_for(j)) if tiles_for else pl.ds(0, src.shape[0])
                copy = pltpu.make_async_remote_copy(
                    src_ref=src.at[tiles], dst_ref=dst.at[1 - dx, gy, tiles], send_sem=send.at[1 - dx, j],
                    recv_sem=recv.at[1 - dx, j], device_id=place(dx, j), device_id_type=MESH)
                copies.append((copy, dx))
        return copies

    def right_side_tiles(j):
        if j == 1:
            return 1, 2
        return (0, 2) if j == gyn - 1 else (1, 1)

    def sum_copies(src, dst, send, recv, count, along_x):
        copies = []
        for j in range(1, count):
            to = (lax.rem(gx + j, gxn), gy) if along_x else (gx, lax.rem(gy + j, gyn))
            copy = pltpu.make_async_remote_copy(
                src_ref=src, dst_ref=dst.at[j], send_sem=send.at[j], recv_sem=recv.at[j],
                device_id=to, device_id_type=MESH)
            copies.append((copy, 0))
        return copies

    def each(copies, do, sign):
        for side, there in ((0, None), (-1, has_w), (1, has_e)):
            group = [copy for copy, dx in copies if dx * sign == side]
            if not group:
                continue
            if there is None:
                for copy in group:
                    do(copy)
            else:
                @pl.when(there)
                def _():
                    for copy in group:
                        do(copy)

    def start(copies):
        each(copies, lambda copy: copy.start(), 1)

    def arrive(copies):
        each(copies, lambda copy: copy.wait_recv(), -1)

    def sent(copies):
        each(copies, lambda copy: copy.wait_send(), 1)

    def extended(k, block, from_w, from_e, from_n, from_s):
        left = jnp.concatenate([from_w[k], block, from_e[k]], axis=0)
        back = (16 - (k % 16)) % 16 * 8
        where = k // 16
        north, south = roll(from_n[where], back, 1), roll(from_s[where], back, 1)
        right = jnp.where(lane24 < 8, north, jnp.where(lane24 >= 120, south, 0.0))
        return jnp.concatenate([left, right], axis=1)

    def layers(body, count=depth):
        for k in range(count):
            body(k)

    def gather_layers(body, carry):
        for k in range(depth):
            carry = body(k, carry)
        return carry

    def get(ref, k, low=0, count=ROWS, shift=0):
        rows = pl.ds(8 + ROWS * k + low + shift, count)
        return jnp.concatenate([ref[0, rows], ref[1, rows]], axis=1)

    def put(ref, k, field, low=0):
        rows = pl.ds(8 + ROWS * k + low, field.shape[0])
        ref[0, rows] = field[:, :128]
        ref[1, rows] = field[:, 128:]

    def mine_of(ref, k):
        return ref[0, pl.ds(8 + ROWS * k + 8, 8)]

    def below_of(k):
        return max(k - 1, 0)

    def above_of(k):
        return min(k + 1, last)

    def first_copies(group, count):
        rows = pl.ds(0, count)
        return halo_copies(msg0.at[group, rows], pack0.at[group], recv0_w.at[group, rows], recv0_e.at[group, rows],
                           recv0_n.at[group], recv0_s.at[group], s0.at[group], r0.at[group])

    def first_ext(group, k):
        return extended(k, msg0[group, k], recv0_w.at[group], recv0_e.at[group], recv0_n.at[group], recv0_s.at[group])

    fetches[0].wait()

    def stage(k):
        msg0[0, k] = soil[k].astype(jnp.float32)
        put_edges(pack0.at[0], k, msg0[0, k])
    layers(stage)
    for fetch in fetches[1:]:
        fetch.wait()
    layers(lambda k: put_edges(pack0.at[1], k, msg0[1, k]))
    layers(lambda k: put_edges(pack0.at[2], k, msg0[2, k]), depth + 1)
    pl.semaphore_wait(barrier, gyn * strips - 1 + gxn - strips)
    groups = [first_copies(0, depth), first_copies(1, depth), first_copies(2, depth + 1)]
    for group in groups:
        start(group)

    valid = (
        ((row_e >= 8) | has_w) & ((row_e < 16) | has_e)
        & ((lane_e < 128) | ((lane_e < 136) & has_n) | ((lane_e >= 248) & has_s))
    )
    arrive(groups[0])

    def look_up(k):
        kinds = first_ext(0, k)
        values = [jnp.zeros((ROWS, LANES), jnp.float32) for _ in range(4)]
        for kind in range(ksat.shape[0]):
            here = kinds == float(kind)
            values = [jnp.where(here, table[kind], value) for table, value in zip((ksat, alpha_t, porosity_t, residual_t), values)]
        con[k] = jnp.where(valid, values[0], 0.0)
        alp[k], por[k], res[k] = values[1], values[2], values[3]
    layers(look_up)
    arrive(groups[1])

    def unpack_pressure(k):
        old[k] = first_ext(1, k)
        state[k] = old[k]
    layers(unpack_pressure)
    arrive(groups[2])

    def unpack_saturation(k):
        sat[k] = first_ext(2, k)
    layers(unpack_saturation)
    rch[...] = first_ext(2, depth)
    for group in groups:
        sent(group)

    def pulled(level, ref, k, field, step, low, count):
        faces = [get(level.at[f], k, low, count) for f in range(2, 8)]
        total = faces[0] * get(ref, k, low, count, -step) + faces[1] * get(ref, k, low, count, step)
        total = total + faces[2] * roll(field, step, 1) + faces[3] * roll(field, -step, 1)
        total = total + faces[4] * get(ref, below_of(k), low, count)
        return total + faces[5] * get(ref, above_of(k), low, count)

    def residual(level, ref, rhs, k, step, low=0, count=ROWS):
        field = get(ref, k, low, count)
        around = pulled(level, ref, k, field, step, low, count)
        return field, get(rhs, k, low, count) - get(level.at[0], k, low, count) * field + around

    def sweep(level, src, rhs, dst, step, low=0, count=ROWS):
        def body(k):
            field, left = residual(level, src, rhs, k, step, low, count)
            put(dst, k, field + get(level.at[1], k, low, count) * left, low)
        layers(body)

    def round_copies(nt, turn, count):
        rows = pl.ds(0, count)
        return halo_copies(msg.at[nt, turn, rows], pack.at[nt, turn], recv_w.at[nt, turn, rows], recv_e.at[nt, turn, rows],
                           recv_n.at[nt, turn], recv_s.at[nt, turn], sh.at[nt, turn], rh.at[nt, turn])

    def round_ext(nt, turn, k):
        return extended(k, msg[nt, turn, k], recv_w.at[nt, turn], recv_e.at[nt, turn],
                        recv_n.at[nt, turn], recv_s.at[nt, turn])

    def precondition(nt, j, rhs, operator):
        def begin(k):
            put(xa, k, get(lev0.at[1], k) * get(rhs, k))
        layers(begin)
        sweep(lev0, xa, rhs, xb, 1)

        def down(k):
            _, left = residual(lev0, xb, rhs, k, 1, 4, 16)
            total = sum_four(left, 1)
            put(b1, k, total, 4)
            put(ya, k, get(lev1.at[1], k, 4, 16) * total, 4)
        layers(down)
        sweep(lev1, ya, b1, yb, 2, 4, 16)
        turn = 2 * j

        def stage_middle(i):
            pair_of = []
            for k in (i, i + half):
                pair_of.append(jnp.where((row8 & 1) == 0, mine_of(yb, k), mine_of(b1, k)))
            mix = jnp.where((lane8 & 1) == 0, pair_of[0], pair_of[1])
            msg[nt, turn, i] = mix
            put_edges(pack.at[nt, turn], i, mix)
        layers(stage_middle, half)
        rows = pl.ds(0, half)
        halo = halo_copies(
            msg.at[nt, turn, rows], pack.at[nt, turn], recv_w.at[nt, turn, rows], recv_e.at[nt, turn, rows],
            recv_n.at[nt, turn], recv_s.at[nt, turn], sh.at[nt, turn], rh.at[nt, turn], True)
        start(halo)

        def deep(k, packed):
            _, left = residual(lev1, yb, b1, k, 2, 8, 8)
            return jnp.where(slot8 == k, sum_four(left[:, :128], 2), packed)
        packed = gather_layers(deep, jnp.zeros(TILE, jnp.float32))
        rhs_out[nt, j, 0] = pack[nt, turn, 0, 0]
        rhs_out[nt, j, 1] = packed
        rhs_out[nt, j, 2] = pack[nt, turn, 1, 0]
        rhs_in[nt, j, 1, gy, 1] = packed
        gathers = gather_copies(rhs_out.at[nt, j], rhs_in.at[nt, j], sb.at[nt, j], rb.at[nt, j], right_side_tiles)
        start(gathers)

        def strips_of(pick):
            return jnp.concatenate(
                [jnp.concatenate([pick(s, y) for y in range(gyn)], axis=1) for s in range(3)], axis=0)

        width = 128 * gyn
        wide_lane, wide_row = iota((ROWS, width), 1), iota((ROWS, width), 0)

        def strip_totals(field):
            total = field[:, :128]
            for y in range(1, gyn):
                total = total + field[:, 128 * y:128 * (y + 1)]
            for step in (4, 8, 16, 32, 64):
                total = total + roll(total, step, 1)
            return sum_pair(total, 4, 0)

        def beneath(e):
            return jnp.where((wide_lane & 3) == 0, roll(roll(e, 1, 0), -3, 1), roll(e, 1, 1))

        def over(e):
            return jnp.where((wide_lane & 3) == 3, roll(roll(e, -1, 0), 3, 1), roll(e, -1, 1))

        if operator is not None:
            arrive(operator)
            diag, south, lower, mixed = (strips_of(lambda s, y: coarse_in[nt, s, y, f]) for f in range(4))
            live = diag > 0.0
            first_row = (wide_row & 4) == 0
            strip[0] = diag
            strip[1] = jnp.where(live, OMEGA / jnp.where(live, diag, 1.0), 0.0)
            strip[2] = jnp.where(first_row, 0.0, roll(mixed, 4, 0))
            strip[3] = jnp.where(first_row, mixed, 0.0)
            strip[4], strip[5] = south, roll(south, -4, 1)
            strip[6], strip[7] = lower, over(lower)
            strip_sum[...] = strip_totals(jnp.where(first_row, 0.0, mixed))
        arrive(gathers)
        b2 = strips_of(lambda s, y: rhs_in[nt, j, s, y, 1])
        below_sum = strip_sum[...]
        some = below_sum > 0.0
        mean = jnp.where(some, strip_totals(b2) / jnp.where(some, below_sum, 1.0), 0.0)

        def coarse_sweep(_, e):
            total = b2 - strip[0] * e
            total = total + strip[2] * roll(e, 4, 0) + strip[3] * roll(e, -4, 0)
            total = total + strip[4] * roll(e, 4, 1) + strip[5] * roll(e, -4, 1)
            total = total + strip[6] * beneath(e) + strip[7] * over(e)
            return e + strip[1] * total
        e2 = lax.fori_loop(0, COARSE_SWEEPS, coarse_sweep, jnp.concatenate([mean] * gyn, axis=1), unroll=True)
        for y in range(gyn):
            solved[y] = e2[:, 128 * y:128 * (y + 1)]
        right = jnp.where(lane24 < 64, solved[jnp.minimum(gy + 1, gyn - 1)], solved[jnp.maximum(gy - 1, 0)])
        around = jnp.concatenate([solved[gy], right], axis=1)
        slot_e = (row_e & 3) * 4 + (lane_e & 3)
        arrive(halo)

        north, south = lax.rem(gy + 1, gyn), lax.rem(gy + gyn - 1, gyn)
        from_n = [jnp.concatenate([rhs_in[nt, j, s, north, 0] for s in range(3)], axis=0)]
        from_s = [jnp.concatenate([rhs_in[nt, j, s, south, 2] for s in range(3)], axis=0)]

        def up(i):
            mix = extended(i, msg[nt, turn, i], recv_w.at[nt, turn], recv_e.at[nt, turn], from_n, from_s)
            for k, low in ((i, True), (i + half, False)):
                def place_layer():
                    m = jnp.where(slot_e == k, around, 0.0)
                    m = roll(m, -(k & 3), 1)
                    m = m + roll(m, 1, 1)
                    m = m + roll(m, 2, 1)
                    m = roll(m, -(k >> 2), 0)
                    m = m + roll(m, 1, 0)
                    m = m + roll(m, 2, 0)
                    both = spread_low(mix, 1, 1) if low else spread_high(mix, 1, 1)
                    put(ya, k, m + jnp.where(even_row, both, roll(both, 1, 0)))
                    put(b1, k, jnp.where(even_row, roll(both, -1, 0), both))
                place_layer()
        layers(up, half)
        sweep(lev1, ya, b1, yb, 2)

        def join(k):
            field, left = residual(lev1, yb, b1, k, 2, 4, 16)
            put(xb, k, get(xb, k, 4, 16) + field + get(lev1.at[1], k, 4, 16) * left, 4)
        layers(join)
        sweep(lev0, xb, rhs, xa, 1, 4, 16)
        sweep(lev0, xa, rhs, xb, 1, 4, 16)
        sent(gathers)
        sent(halo)

    def applied(k):
        field = get(xb, k, 8, 8)
        return (get(lev0.at[0], k, 8, 8) * field - pulled(lev0, xb, k, field, 1, 8, 8))[:, :128]

    def newton(nt, carry):
        def cells(k):
            effective = 1.0 / (1.0 + jnp.exp(-(alp[k] * state[k])))
            saturation = res[k] + (1.0 - res[k]) * effective
            slope = (1.0 - res[k]) * alp[k] * effective * (1.0 - effective)
            rel[k] = effective * effective
            stored[k] = STORAGE + por[k] * slope
            put(g, k, por[k] * (saturation - sat[k]) + STORAGE * (state[k] - old[k]))
        layers(cells)

        def faces(k):
            def face(con_n, rel_n):
                total = con[k] + con_n
                live = total > 0.0
                return 2.0 * con[k] * con_n / jnp.where(live, total, 1.0) * (0.5 * (rel[k] + rel_n))
            west = face(roll(con[k], 1, 0), roll(rel[k], 1, 0))
            south = face(roll(con[k], 1, 1), roll(rel[k], 1, 1))
            lower = face(con[k - 1], rel[k - 1]) if k else jnp.zeros((ROWS, LANES), jnp.float32)
            for f, field in enumerate((west, roll(west, -1, 0), south, roll(south, -1, 1), lower)):
                put(lev0.at[f + 2], k, field)
        layers(faces)

        def operators(k, carried):
            middle_lower, packed = carried
            west, east, south, north, lower = (get(lev0.at[f], k) for f in range(2, 7))
            upper = get(lev0.at[6], k + 1) if k < last else jnp.zeros((ROWS, LANES), jnp.float32)
            put(lev0.at[7], k, upper)
            diag = stored[k] + west + east + south + north + lower + upper
            put(lev0.at[0], k, diag)
            put(lev0.at[1], k, OMEGA / diag)
            here = state[k]
            below, above = state[below_of(k)], state[above_of(k)]
            flux = (
                west * (here - roll(here, 1, 0)) + east * (here - roll(here, -1, 0))
                + south * (here - roll(here, 1, 1)) + north * (here - roll(here, -1, 1))
                + lower * (here - below + 1.0) + upper * (here - above - 1.0)
            )
            gain = rch[...] - get(g, k) if k == last else -get(g, k)
            put(g, k, gain - flux)
            middle_west = spread_low(sum_pair(west, 1, 1), 1, 0)
            middle_south = spread_low(sum_pair(south, 1, 0), 1, 1)
            middle_upper = sum_four(upper, 1)
            middle = (sum_four(stored[k], 1), middle_west, roll(middle_west, -2, 0), middle_south,
                      roll(middle_south, -2, 1), middle_lower, middle_upper)
            diag = middle[0]
            for f in range(1, 7):
                put(lev1.at[f + 1], k, middle[f])
                diag = diag + middle[f]
            put(lev1.at[0], k, diag)
            put(lev1.at[1], k, OMEGA / diag)
            coarse = coarsen([field[8:16, :128] for field in middle], 2)
            diag = coarse[0]
            for f in range(1, 7):
                diag = diag + coarse[f]
            mixed = jnp.where((row8 & 4) == 0, coarse[2], sum_pair(coarse[0], 4, 0))
            return middle_upper, tuple(jnp.where(slot8 == k, field, so_far)
                                       for field, so_far in zip((diag, coarse[3], coarse[5], mixed), packed))
        _, packed = gather_layers(operators, (jnp.zeros((ROWS, LANES), jnp.float32), (jnp.zeros(TILE, jnp.float32),) * 4))
        for f in range(4):
            coarse_out[nt, f] = packed[f]
            coarse_in[nt, 1, gy, f] = packed[f]
        operator = gather_copies(coarse_out.at[nt], coarse_in.at[nt], sc.at[nt], rc.at[nt])
        start(operator)
        precondition(nt, 0, g, operator)

        zeros = jnp.zeros(TILE, jnp.float32)

        def image(k, sums):
            gg, gp, pp = sums
            mine = mine_of(g, k)
            diff = applied(k) - mine
            z0[k] = mine_of(xb, k)
            msg[nt, 3, k] = z0[k]
            put_edges(pack.at[nt, 3], k, z0[k])
            own[k] = diff
            msg[nt, 1, k] = diff
            put_edges(pack.at[nt, 1], k, diff)
            return gg + mine * mine, gp + mine * diff, pp + diff * diff
        gg, gp, pp = gather_layers(image, (zeros, zeros, zeros))
        halo = round_copies(nt, 1, depth)
        halo_z = round_copies(nt, 3, depth)
        halo_u = round_copies(nt, 4, depth)
        start(halo)
        arrive(halo)

        @pl.when(nt < NEWTON - 1)
        def _():
            start(halo_z)

        def spread(k):
            put(b0, k, round_ext(nt, 1, k))
        layers(spread)
        sent(halo)
        precondition(nt, 1, b0, None)

        def second(k, sums):
            gs, ps, ss = sums
            mine = mine_of(g, k)
            im = applied(k)
            u = mine_of(xb, k)
            msg[nt, 4, k] = u
            put_edges(pack.at[nt, 4], k, u)
            return gs + mine * im, ps + own[k] * im, ss + im * im
        gs, ps, ss = gather_layers(second, (zeros, zeros, zeros))

        rows = [jnp.sum(item, axis=0, keepdims=True) for item in (gg, gp, pp, gs, ps, ss)]
        tile = zeros
        for i, item in enumerate(rows):
            tile = jnp.where(row8 == i, jnp.broadcast_to(item, TILE), tile)
        part_out[nt] = tile
        along_y = sum_copies(part_out.at[nt], part_y.at[nt], sy.at[nt], ry.at[nt], gyn, False)
        start(along_y)

        @pl.when(nt < NEWTON - 1)
        def _():
            start(halo_u)
        arrive(along_y)
        for j in range(1, gyn):
            tile = tile + part_y[nt, j]
        whole_x[nt] = tile
        along_x = sum_copies(whole_x.at[nt], part_x.at[nt], sx.at[nt], rx.at[nt], gxn, True)
        start(along_x)
        arrive(along_x)
        for j in range(1, gxn):
            tile = tile + part_x[nt, j]
        totals = jnp.broadcast_to(jnp.sum(tile, axis=1, keepdims=True), (8, LANES))
        gg, gp, pp, gs, ps, ss = (totals[i:i + 1] for i in range(6))

        square = gg + EPSILON
        beta = jnp.sqrt(square)
        h00 = (gg + gp) / square
        a = (EPSILON - gp) / square
        vv = jnp.maximum(pp + 2.0 * a * gp + a * a * gg, 0.0)
        h10 = jnp.sqrt(vv / square + EPSILON)
        kappa = 1.0 / (beta * h10)
        gw = gs + a * gp + a * gg
        h01 = kappa / beta * gw
        h11 = kappa * kappa * (ps + a * pp + a * gp + a * gw)
        ww = kappa * kappa * (ss + 2.0 * a * (ps + gs) + a * a * (pp + 2.0 * gp + gg))
        v00 = gg / square
        v11 = kappa * kappa * vv
        v01 = kappa / beta * (gp + a * gg)
        rest = ww - h01 * h01 * (2.0 - v00) - h11 * h11 * (2.0 - v11) + 2.0 * h01 * h11 * v01
        h21_sq = jnp.maximum(rest, 0.0) + EPSILON
        m00 = h00 * h00 + h10 * h10
        m01 = h00 * h01 + h10 * h11
        m11 = h01 * h01 + h11 * h11 + h21_sq
        q0, q1 = beta * h00, beta * h01
        factor = m01 / m00
        y1 = (q1 - factor * q0) / (m11 - factor * m01)
        y0 = (q0 - m01 * y1) / m00
        first_weight = y0 / beta + y1 * kappa * a
        second_weight = y1 * kappa

        @pl.when(nt < NEWTON - 1)
        def _():
            arrive(halo_z)
            arrive(halo_u)

            def advance(k):
                state[k] = state[k] + first_weight * round_ext(nt, 3, k) + second_weight * round_ext(nt, 4, k)
            layers(advance)
            sent(halo_z)
            sent(halo_u)

        @pl.when(nt == NEWTON - 1)
        def _():
            def finish(k):
                out[k] = (state[k][8:16, :128] + first_weight[:, :128] * z0[k]
                          + second_weight[:, :128] * msg[nt, 4, k])
            layers(finish)
        sent(operator)
        sent(along_y)
        sent(along_x)
        return carry

    lax.fori_loop(0, NEWTON, newton, 0)


def on_device(gxn, gyn, *args):
    depth = args[0].shape[0]

    def vmem(*shape):
        return pltpu.VMEM(shape, jnp.float32)

    def dma(*shape):
        return pltpu.SemaphoreType.DMA(shape)

    ext = vmem(depth, ROWS, LANES)
    flat = ROWS * depth + 16
    level = vmem(8, 2, flat, 128)
    n0 = depth + 1
    assert n0 <= 16
    scratch = [ext] * 7 + [vmem(ROWS, LANES), ext, ext]
    scratch += [level, level] + [vmem(2, flat, 128)] * 7 + [vmem(depth, *TILE)]
    scratch += [pltpu.VMEM((depth,) + TILE, jnp.int32)] + [pltpu.SMEM(item.shape, jnp.float32) for item in args[4:]]
    scratch += [
        vmem(depth, *TILE), vmem(3, n0, *TILE), vmem(3, n0, *TILE), vmem(3, n0, *TILE),
        vmem(3, 2, 1, *TILE), vmem(3, 1, ROWS, 128), vmem(3, 1, ROWS, 128),
        vmem(NEWTON, HALO, depth, *TILE), vmem(NEWTON, HALO, depth, *TILE), vmem(NEWTON, HALO, depth, *TILE),
        vmem(NEWTON, HALO, 2, 1, *TILE), vmem(NEWTON, HALO, 1, ROWS, 128), vmem(NEWTON, HALO, 1, ROWS, 128),
        vmem(NEWTON, 4, *TILE), vmem(NEWTON, 3, gyn, 4, *TILE), vmem(NEWTON, 2, 3, *TILE), vmem(NEWTON, 2, 3, gyn, 3, *TILE),
        vmem(8, ROWS, 128 * gyn), vmem(ROWS, 128), vmem(gyn, ROWS, 128),
        vmem(NEWTON, *TILE), vmem(NEWTON, gyn, *TILE), vmem(NEWTON, gxn, *TILE), vmem(NEWTON, *TILE),
        dma(8), dma(3, 8), dma(3, 8), dma(NEWTON, HALO, 8), dma(NEWTON, HALO, 8),
        dma(NEWTON, 3, gyn), dma(NEWTON, 3, gyn), dma(NEWTON, 2, 3, gyn), dma(NEWTON, 2, 3, gyn),
        dma(NEWTON, gyn), dma(NEWTON, gyn), dma(NEWTON, gxn), dma(NEWTON, gxn),
    ]
    return pl.pallas_call(
        functools.partial(kernel, gxn, gyn, depth),
        out_shape=jax.ShapeDtypeStruct(args[0].shape, jnp.float32),
        in_specs=[pl.BlockSpec(memory_space=pltpu.HBM)] * 8,
        out_specs=pl.BlockSpec(memory_space=pltpu.VMEM),
        scratch_shapes=scratch,
        compiler_params=pltpu.CompilerParams(
            collective_id=0, has_side_effects=True, vmem_limit_bytes=64 * 1024 * 1024),
    )(*args)


def solution(mesh):
    cells = P(None, "gx", "gy")
    placed = (cells, cells, cells, P("gx", "gy"), P(), P(), P(), P())
    return jax.shard_map(
        functools.partial(on_device, mesh.shape["gx"], mesh.shape["gy"]),
        mesh=mesh, in_specs=placed, out_specs=cells, check_vma=False,
    )
```

```python
import functools

import jax
import jax.numpy as jnp
from jax import lax
from jax.experimental import pallas as pl
from jax.experimental.pallas import tpu as pltpu
from jax.sharding import PartitionSpec as P

NEWTON = 2
COARSE_SWEEPS = 4
OMEGA = 0.8
STORAGE = 0.05
EPSILON = 1e-06

ROWS = 24
LANES = 256
TILE = (8, 128)
MESH = pl.DeviceIdType.MESH
DIRECTIONS = tuple((dx, dy) for dx in (-1, 0, 1) for dy in (-1, 0, 1) if (dx, dy) != (0, 0))
HALO = 5


def roll(field, shift, axis):
    size = field.shape[axis]
    return pltpu.roll(field, shift % size if isinstance(shift, int) else shift, axis)


def iota(shape, axis):
    return lax.broadcasted_iota(jnp.int32, shape, axis)


def pair(field, step, axis):
    low = (iota(field.shape, axis) & step) == 0
    return jnp.where(low, roll(field, -step, axis), roll(field, step, axis))


def sum_pair(field, step, axis):
    return field + pair(field, step, axis)


def sum_four(field, step):
    return sum_pair(sum_pair(field, step, 1), step, 0)


def spread_low(field, step, axis):
    low = (iota(field.shape, axis) & step) == 0
    return jnp.where(low, field, roll(field, step, axis))


def spread_high(field, step, axis):
    low = (iota(field.shape, axis) & step) == 0
    return jnp.where(low, roll(field, -step, axis), field)


def coarsen(coefs, step):
    storage, west, east, south, north, lower, upper = coefs
    return (
        sum_four(storage, step),
        spread_low(sum_pair(west, step, 1), step, 0),
        spread_high(sum_pair(east, step, 1), step, 0),
        spread_low(sum_pair(south, step, 0), step, 1),
        spread_high(sum_pair(north, step, 0), step, 1),
        sum_four(lower, step),
        sum_four(upper, step),
    )


def kernel(
    gxn, gyn, depth,
    pressure, saturation_old, soil_type, recharge, ksat_in, alpha_in, porosity_in, residual_in,
    out,
    old, state, sat, con, alp, por, res, rch, rel, stored,
    lev0, lev1, g, b0, xa, xb, b1, ya, yb, z0,
    soil, ksat, alpha_t, porosity_t, residual_t,
    own, msg0, recv0_w, recv0_e, pack0, recv0_n, recv0_s,
    msg, recv_w, recv_e, pack, recv_n, recv_s,
    coarse_out, coarse_in, rhs_out, rhs_in, strip, strip_sum, solved,
    part_out, part_in,
    local, s0, r0, sh, rh, sc, rc, sb, rb, sx, rx,
):
    gx, gy = lax.axis_index("gx"), lax.axis_index("gy")
    has_w, has_e = gx > 0, gx < gxn - 1
    has_s, has_n = gy > 0, gy < gyn - 1
    last = depth - 1

    def inside(dx, dy):
        x, y = gx + dx, gy + dy
        return (x >= 0) & (x < gxn) & (y >= 0) & (y < gyn)

    def place(dx, dy):
        return (jnp.clip(gx + dx, 0, gxn - 1), jnp.clip(gy + dy, 0, gyn - 1))

    assert depth % 2 == 0
    half = depth // 2
    fetches = [
        pltpu.make_async_copy(src, dst, local.at[i])
        for i, (src, dst) in enumerate((
            (soil_type, soil), (pressure, msg0.at[1, pl.ds(0, depth)]),
            (saturation_old, msg0.at[2, pl.ds(0, depth)]), (recharge, msg0.at[2, depth]),
            (ksat_in, ksat), (alpha_in, alpha_t), (porosity_in, porosity_t), (residual_in, residual_t)))
    ]
    for fetch in fetches:
        fetch.start()

    for ref in (xa, xb, ya, yb):
        for h in range(2):
            ref[h, pl.ds(0, 8)] = jnp.zeros(TILE, jnp.float32)
            ref[h, pl.ds(8 + ROWS * depth, 8)] = jnp.zeros(TILE, jnp.float32)
    for ref in (recv0_w, recv0_e, recv0_n, recv0_s, recv_w, recv_e, recv_n, recv_s,
                coarse_in, rhs_in, pack0, pack):
        ref[...] = jnp.zeros(ref.shape, ref.dtype)

    barrier = pltpu.get_barrier_semaphore()
    others = [(i, j) for i in range(gxn) for j in range(gyn) if (i, j) != (0, 0)]

    def around_by(i, j):
        return (lax.rem(gx + i, gxn), lax.rem(gy + j, gyn))

    for i, j in others:
        pl.semaphore_signal(barrier, inc=1, device_id=around_by(i, j), device_id_type=MESH)

    lane8, row8 = iota(TILE, 1), iota(TILE, 0)
    slot8 = (row8 & 3) * 4 + (lane8 & 3)
    lane_e, row_e = iota((ROWS, LANES), 1), iota((ROWS, LANES), 0)
    lane24 = iota((ROWS, 128), 1)
    even_row = (row_e & 1) == 0

    def put_edges(packs, k, block):
        at = (k % 16)
        moved = roll(block, at * 8, 1)
        group = lane8 >> 3
        where = k // 16
        packs[0, where] = jnp.where(group == at, moved, packs[0, where])
        packs[1, where] = jnp.where(group == ((at + 15) % 16), moved, packs[1, where])

    def halo_copies(blocks, packs, to_w, to_e, to_n, to_s, send, recv):
        copies = []
        for d, (dx, dy) in enumerate(DIRECTIONS):
            rows = pl.ds(8 * (1 - dx), 8)
            if dy == 0:
                src, dst = blocks, (to_w if dx > 0 else to_e)
            elif dy > 0:
                src, dst = packs.at[1], to_s.at[:, rows]
            else:
                src, dst = packs.at[0], to_n.at[:, rows]
            copy = pltpu.make_async_remote_copy(
                src_ref=src, dst_ref=dst, send_sem=send.at[d], recv_sem=recv.at[d],
                device_id=place(dx, dy), device_id_type=MESH)
            copies.append((copy, inside(dx, dy), inside(-dx, -dy)))
        return copies

    def gather_copies(src, dst, send, recv):
        copies = []
        for dx in (-1, 0, 1):
            for j in range(gyn):
                if (dx, j) == (0, 0):
                    continue
                copy = pltpu.make_async_remote_copy(
                    src_ref=src, dst_ref=dst.at[1 - dx, gy], send_sem=send.at[1 - dx, j], recv_sem=recv.at[1 - dx, j],
                    device_id=(jnp.clip(gx + dx, 0, gxn - 1), lax.rem(gy + j, gyn)), device_id_type=MESH)
                copies.append((copy, inside(dx, 0), inside(-dx, 0)))
        return copies

    def sum_copies(src, dst, send, recv):
        copies = []
        for i, j in others:
            copy = pltpu.make_async_remote_copy(
                src_ref=src, dst_ref=dst.at[i * gyn + j], send_sem=send.at[i, j], recv_sem=recv.at[i, j],
                device_id=around_by(i, j), device_id_type=MESH)
            copies.append((copy, None, None))
        return copies

    def each(copies, do, which):
        for entry in copies:
            if entry[which] is None:
                do(entry[0])
            else:
                @pl.when(entry[which])
                def _():
                    do(entry[0])

    def start(copies):
        each(copies, lambda copy: copy.start(), 1)

    def arrive(copies):
        each(copies, lambda copy: copy.wait_recv(), 2)

    def sent(copies):
        each(copies, lambda copy: copy.wait_send(), 1)

    def extended(k, block, from_w, from_e, from_n, from_s):
        left = jnp.concatenate([from_w[k], block, from_e[k]], axis=0)
        back = (16 - (k % 16)) % 16 * 8
        where = k // 16
        north, south = roll(from_n[where], back, 1), roll(from_s[where], back, 1)
        right = jnp.where(lane24 < 8, north, jnp.where(lane24 >= 120, south, 0.0))
        return jnp.concatenate([left, right], axis=1)

    def layers(body, count=depth):
        for k in range(count):
            body(k)

    def gather_layers(body, carry):
        for k in range(depth):
            carry = body(k, carry)
        return carry

    def get(ref, k, low=0, count=ROWS, shift=0):
        rows = pl.ds(8 + ROWS * k + low + shift, count)
        return jnp.concatenate([ref[0, rows], ref[1, rows]], axis=1)

    def put(ref, k, field, low=0):
        rows = pl.ds(8 + ROWS * k + low, field.shape[0])
        ref[0, rows] = field[:, :128]
        ref[1, rows] = field[:, 128:]

    def mine_of(ref, k):
        return ref[0, pl.ds(8 + ROWS * k + 8, 8)]

    def below_of(k):
        return max(k - 1, 0)

    def above_of(k):
        return min(k + 1, last)

    def first_copies(group, count):
        rows = pl.ds(0, count)
        return halo_copies(msg0.at[group, rows], pack0.at[group], recv0_w.at[group, rows], recv0_e.at[group, rows],
                           recv0_n.at[group], recv0_s.at[group], s0.at[group], r0.at[group])

    def first_ext(group, k):
        return extended(k, msg0[group, k], recv0_w.at[group], recv0_e.at[group], recv0_n.at[group], recv0_s.at[group])

    fetches[0].wait()

    def stage(k):
        msg0[0, k] = soil[k].astype(jnp.float32)
        put_edges(pack0.at[0], k, msg0[0, k])
    layers(stage)
    for fetch in fetches[1:]:
        fetch.wait()
    layers(lambda k: put_edges(pack0.at[1], k, msg0[1, k]))
    layers(lambda k: put_edges(pack0.at[2], k, msg0[2, k]), depth + 1)
    pl.semaphore_wait(barrier, len(others))
    groups = [first_copies(0, depth), first_copies(1, depth), first_copies(2, depth + 1)]
    for group in groups:
        start(group)

    valid = (
        ((row_e >= 8) | has_w) & ((row_e < 16) | has_e)
        & ((lane_e < 128) | ((lane_e < 136) & has_n) | ((lane_e >= 248) & has_s))
    )
    arrive(groups[0])

    def look_up(k):
        kinds = first_ext(0, k)
        values = [jnp.zeros((ROWS, LANES), jnp.float32) for _ in range(4)]
        for kind in range(ksat.shape[0]):
            here = kinds == float(kind)
            values = [jnp.where(here, table[kind], value) for table, value in zip((ksat, alpha_t, porosity_t, residual_t), values)]
        con[k] = jnp.where(valid, values[0], 0.0)
        alp[k], por[k], res[k] = values[1], values[2], values[3]
    layers(look_up)
    arrive(groups[1])

    def unpack_pressure(k):
        old[k] = first_ext(1, k)
        state[k] = old[k]
    layers(unpack_pressure)
    arrive(groups[2])

    def unpack_saturation(k):
        sat[k] = first_ext(2, k)
    layers(unpack_saturation)
    rch[...] = first_ext(2, depth)
    for group in groups:
        sent(group)

    def pulled(level, ref, k, field, step, low, count):
        faces = [get(level.at[f], k, low, count) for f in range(2, 8)]
        total = faces[0] * get(ref, k, low, count, -step) + faces[1] * get(ref, k, low, count, step)
        total = total + faces[2] * roll(field, step, 1) + faces[3] * roll(field, -step, 1)
        total = total + faces[4] * get(ref, below_of(k), low, count)
        return total + faces[5] * get(ref, above_of(k), low, count)

    def residual(level, ref, rhs, k, step, low=0, count=ROWS):
        field = get(ref, k, low, count)
        around = pulled(level, ref, k, field, step, low, count)
        return field, get(rhs, k, low, count) - get(level.at[0], k, low, count) * field + around

    def sweep(level, src, rhs, dst, step, low=0, count=ROWS):
        def body(k):
            field, left = residual(level, src, rhs, k, step, low, count)
            put(dst, k, field + get(level.at[1], k, low, count) * left, low)
        layers(body)

    def round_copies(nt, turn, count):
        rows = pl.ds(0, count)
        return halo_copies(msg.at[nt, turn, rows], pack.at[nt, turn], recv_w.at[nt, turn, rows], recv_e.at[nt, turn, rows],
                           recv_n.at[nt, turn], recv_s.at[nt, turn], sh.at[nt, turn], rh.at[nt, turn])

    def round_ext(nt, turn, k):
        return extended(k, msg[nt, turn, k], recv_w.at[nt, turn], recv_e.at[nt, turn],
                        recv_n.at[nt, turn], recv_s.at[nt, turn])

    def precondition(nt, j, rhs, operator):
        def begin(k):
            put(xa, k, get(lev0.at[1], k) * get(rhs, k))
        layers(begin)
        sweep(lev0, xa, rhs, xb, 1)

        def down(k):
            _, left = residual(lev0, xb, rhs, k, 1, 4, 16)
            total = sum_four(left, 1)
            put(b1, k, total, 4)
            put(ya, k, get(lev1.at[1], k, 4, 16) * total, 4)
        layers(down)
        sweep(lev1, ya, b1, yb, 2, 4, 16)
        turn = 2 * j

        def stage_middle(i):
            pair_of = []
            for k in (i, i + half):
                pair_of.append(jnp.where((row8 & 1) == 0, mine_of(yb, k), mine_of(b1, k)))
            mix = jnp.where((lane8 & 1) == 0, pair_of[0], pair_of[1])
            msg[nt, turn, i] = mix
            put_edges(pack.at[nt, turn], i, mix)
        layers(stage_middle, half)
        halo = round_copies(nt, turn, half)
        start(halo)

        def deep(k, packed):
            _, left = residual(lev1, yb, b1, k, 2, 8, 8)
            return jnp.where(slot8 == k, sum_four(left[:, :128], 2), packed)
        packed = gather_layers(deep, jnp.zeros(TILE, jnp.float32))
        rhs_out[nt, j] = packed
        rhs_in[nt, j, 1, gy] = packed
        gathers = gather_copies(rhs_out.at[nt, j], rhs_in.at[nt, j], sb.at[nt, j], rb.at[nt, j])
        start(gathers)

        def strips_of(pick):
            return jnp.concatenate(
                [jnp.concatenate([pick(s, y) for y in range(gyn)], axis=1) for s in range(3)], axis=0)

        width = 128 * gyn
        wide_lane, wide_row = iota((ROWS, width), 1), iota((ROWS, width), 0)

        def strip_totals(field):
            total = field[:, :128]
            for y in range(1, gyn):
                total = total + field[:, 128 * y:128 * (y + 1)]
            for step in (4, 8, 16, 32, 64):
                total = total + roll(total, step, 1)
            return sum_pair(total, 4, 0)

        def beneath(e):
            return jnp.where((wide_lane & 3) == 0, roll(roll(e, 1, 0), -3, 1), roll(e, 1, 1))

        def over(e):
            return jnp.where((wide_lane & 3) == 3, roll(roll(e, -1, 0), 3, 1), roll(e, -1, 1))

        if operator is not None:
            arrive(operator)
            diag, south, lower, mixed = (strips_of(lambda s, y: coarse_in[nt, s, y, f]) for f in range(4))
            live = diag > 0.0
            first_row = (wide_row & 4) == 0
            strip[0] = diag
            strip[1] = jnp.where(live, OMEGA / jnp.where(live, diag, 1.0), 0.0)
            strip[2] = jnp.where(first_row, 0.0, roll(mixed, 4, 0))
            strip[3] = jnp.where(first_row, mixed, 0.0)
            strip[4], strip[5] = south, roll(south, -4, 1)
            strip[6], strip[7] = lower, over(lower)
            strip_sum[...] = strip_totals(jnp.where(first_row, 0.0, mixed))
        arrive(gathers)
        b2 = strips_of(lambda s, y: rhs_in[nt, j, s, y])
        below_sum = strip_sum[...]
        some = below_sum > 0.0
        mean = jnp.where(some, strip_totals(b2) / jnp.where(some, below_sum, 1.0), 0.0)

        def coarse_sweep(_, e):
            total = b2 - strip[0] * e
            total = total + strip[2] * roll(e, 4, 0) + strip[3] * roll(e, -4, 0)
            total = total + strip[4] * roll(e, 4, 1) + strip[5] * roll(e, -4, 1)
            total = total + strip[6] * beneath(e) + strip[7] * over(e)
            return e + strip[1] * total
        e2 = lax.fori_loop(0, COARSE_SWEEPS, coarse_sweep, jnp.concatenate([mean] * gyn, axis=1), unroll=True)
        for y in range(gyn):
            solved[y] = e2[:, 128 * y:128 * (y + 1)]
        right = jnp.where(lane24 < 64, solved[jnp.minimum(gy + 1, gyn - 1)], solved[jnp.maximum(gy - 1, 0)])
        around = jnp.concatenate([solved[gy], right], axis=1)
        slot_e = (row_e & 3) * 4 + (lane_e & 3)
        arrive(halo)

        def up(i):
            mix = round_ext(nt, turn, i)
            for k, low in ((i, True), (i + half, False)):
                def place_layer():
                    m = jnp.where(slot_e == k, around, 0.0)
                    m = roll(m, -(k & 3), 1)
                    m = m + roll(m, 1, 1)
                    m = m + roll(m, 2, 1)
                    m = roll(m, -(k >> 2), 0)
                    m = m + roll(m, 1, 0)
                    m = m + roll(m, 2, 0)
                    both = spread_low(mix, 1, 1) if low else spread_high(mix, 1, 1)
                    put(ya, k, m + jnp.where(even_row, both, roll(both, 1, 0)))
                    put(b1, k, jnp.where(even_row, roll(both, -1, 0), both))
                place_layer()
        layers(up, half)
        sweep(lev1, ya, b1, yb, 2)

        def join(k):
            field, left = residual(lev1, yb, b1, k, 2, 4, 16)
            put(xb, k, get(xb, k, 4, 16) + field + get(lev1.at[1], k, 4, 16) * left, 4)
        layers(join)
        sweep(lev0, xb, rhs, xa, 1, 4, 16)
        sweep(lev0, xa, rhs, xb, 1, 4, 16)
        sent(gathers)
        sent(halo)

    def applied(k):
        field = get(xb, k, 8, 8)
        return (get(lev0.at[0], k, 8, 8) * field - pulled(lev0, xb, k, field, 1, 8, 8))[:, :128]

    def newton(nt, carry):
        def cells(k):
            effective = 1.0 / (1.0 + jnp.exp(-(alp[k] * state[k])))
            saturation = res[k] + (1.0 - res[k]) * effective
            slope = (1.0 - res[k]) * alp[k] * effective * (1.0 - effective)
            rel[k] = effective * effective
            stored[k] = STORAGE + por[k] * slope
            put(g, k, por[k] * (saturation - sat[k]) + STORAGE * (state[k] - old[k]))
        layers(cells)

        def faces(k):
            def face(con_n, rel_n):
                total = con[k] + con_n
                live = total > 0.0
                return 2.0 * con[k] * con_n / jnp.where(live, total, 1.0) * (0.5 * (rel[k] + rel_n))
            west = face(roll(con[k], 1, 0), roll(rel[k], 1, 0))
            south = face(roll(con[k], 1, 1), roll(rel[k], 1, 1))
            lower = face(con[k - 1], rel[k - 1]) if k else jnp.zeros((ROWS, LANES), jnp.float32)
            for f, field in enumerate((west, roll(west, -1, 0), south, roll(south, -1, 1), lower)):
                put(lev0.at[f + 2], k, field)
        layers(faces)

        def operators(k, carried):
            middle_lower, packed = carried
            west, east, south, north, lower = (get(lev0.at[f], k) for f in range(2, 7))
            upper = get(lev0.at[6], k + 1) if k < last else jnp.zeros((ROWS, LANES), jnp.float32)
            put(lev0.at[7], k, upper)
            diag = stored[k] + west + east + south + north + lower + upper
            put(lev0.at[0], k, diag)
            put(lev0.at[1], k, OMEGA / diag)
            here = state[k]
            below, above = state[below_of(k)], state[above_of(k)]
            flux = (
                west * (here - roll(here, 1, 0)) + east * (here - roll(here, -1, 0))
                + south * (here - roll(here, 1, 1)) + north * (here - roll(here, -1, 1))
                + lower * (here - below + 1.0) + upper * (here - above - 1.0)
            )
            gain = rch[...] - get(g, k) if k == last else -get(g, k)
            put(g, k, gain - flux)
            middle_west = spread_low(sum_pair(west, 1, 1), 1, 0)
            middle_south = spread_low(sum_pair(south, 1, 0), 1, 1)
            middle_upper = sum_four(upper, 1)
            middle = (sum_four(stored[k], 1), middle_west, roll(middle_west, -2, 0), middle_south,
                      roll(middle_south, -2, 1), middle_lower, middle_upper)
            diag = middle[0]
            for f in range(1, 7):
                put(lev1.at[f + 1], k, middle[f])
                diag = diag + middle[f]
            put(lev1.at[0], k, diag)
            put(lev1.at[1], k, OMEGA / diag)
            coarse = coarsen([field[8:16, :128] for field in middle], 2)
            diag = coarse[0]
            for f in range(1, 7):
                diag = diag + coarse[f]
            mixed = jnp.where((row8 & 4) == 0, coarse[2], sum_pair(coarse[0], 4, 0))
            return middle_upper, tuple(jnp.where(slot8 == k, field, so_far)
                                       for field, so_far in zip((diag, coarse[3], coarse[5], mixed), packed))
        _, packed = gather_layers(operators, (jnp.zeros((ROWS, LANES), jnp.float32), (jnp.zeros(TILE, jnp.float32),) * 4))
        for f in range(4):
            coarse_out[nt, f] = packed[f]
            coarse_in[nt, 1, gy, f] = packed[f]
        operator = gather_copies(coarse_out.at[nt], coarse_in.at[nt], sc.at[nt], rc.at[nt])
        start(operator)
        precondition(nt, 0, g, operator)

        zeros = jnp.zeros(TILE, jnp.float32)

        def image(k, sums):
            gg, gp, pp = sums
            mine = mine_of(g, k)
            diff = applied(k) - mine
            z0[k] = mine_of(xb, k)
            msg[nt, 3, k] = z0[k]
            put_edges(pack.at[nt, 3], k, z0[k])
            own[k] = diff
            msg[nt, 1, k] = diff
            put_edges(pack.at[nt, 1], k, diff)
            return gg + mine * mine, gp + mine * diff, pp + diff * diff
        gg, gp, pp = gather_layers(image, (zeros, zeros, zeros))
        halo = round_copies(nt, 1, depth)
        halo_z = round_copies(nt, 3, depth)
        halo_u = round_copies(nt, 4, depth)
        start(halo)
        arrive(halo)

        @pl.when(nt < NEWTON - 1)
        def _():
            start(halo_z)

        def spread(k):
            put(b0, k, round_ext(nt, 1, k))
        layers(spread)
        sent(halo)
        precondition(nt, 1, b0, None)

        def second(k, sums):
            gs, ps, ss = sums
            mine = mine_of(g, k)
            im = applied(k)
            u = mine_of(xb, k)
            msg[nt, 4, k] = u
            put_edges(pack.at[nt, 4], k, u)
            return gs + mine * im, ps + own[k] * im, ss + im * im
        gs, ps, ss = gather_layers(second, (zeros, zeros, zeros))

        tile = zeros
        for i, item in enumerate((gg, gp, pp, gs, ps, ss)):
            tile = jnp.where(row8 == i, jnp.broadcast_to(jnp.sum(item, axis=0, keepdims=True), TILE), tile)
        for step in (64, 32, 16):
            tile = tile + roll(tile, step, 1)
        own_lanes = (lane8 >> 4) == row8
        part_out[nt] = jnp.sum(jnp.where(own_lanes, tile, 0.0), axis=0, keepdims=True)
        part_in[nt, 0] = part_out[nt]
        sums = sum_copies(part_out.at[nt], part_in.at[nt], sx.at[nt], rx.at[nt])
        start(sums)

        @pl.when(nt < NEWTON - 1)
        def _():
            start(halo_u)
        arrive(sums)
        whole = part_in[nt, 0]
        for i in range(1, gxn * gyn):
            whole = whole + part_in[nt, i]
        tile = jnp.where(own_lanes, jnp.broadcast_to(whole, TILE), 0.0)
        totals = jnp.broadcast_to(jnp.sum(tile, axis=1, keepdims=True), (8, LANES))
        gg, gp, pp, gs, ps, ss = (totals[i:i + 1] for i in range(6))

        square = gg + EPSILON
        beta = jnp.sqrt(square)
        h00 = (gg + gp) / square
        a = (EPSILON - gp) / square
        vv = jnp.maximum(pp + 2.0 * a * gp + a * a * gg, 0.0)
        h10 = jnp.sqrt(vv / square + EPSILON)
        kappa = 1.0 / (beta * h10)
        gw = gs + a * gp + a * gg
        h01 = kappa / beta * gw
        h11 = kappa * kappa * (ps + a * pp + a * gp + a * gw)
        ww = kappa * kappa * (ss + 2.0 * a * (ps + gs) + a * a * (pp + 2.0 * gp + gg))
        v00 = gg / square
        v11 = kappa * kappa * vv
        v01 = kappa / beta * (gp + a * gg)
        rest = ww - h01 * h01 * (2.0 - v00) - h11 * h11 * (2.0 - v11) + 2.0 * h01 * h11 * v01
        h21_sq = jnp.maximum(rest, 0.0) + EPSILON
        m00 = h00 * h00 + h10 * h10
        m01 = h00 * h01 + h10 * h11
        m11 = h01 * h01 + h11 * h11 + h21_sq
        q0, q1 = beta * h00, beta * h01
        factor = m01 / m00
        y1 = (q1 - factor * q0) / (m11 - factor * m01)
        y0 = (q0 - m01 * y1) / m00
        first_weight = y0 / beta + y1 * kappa * a
        second_weight = y1 * kappa

        @pl.when(nt < NEWTON - 1)
        def _():
            arrive(halo_z)
            arrive(halo_u)

            def advance(k):
                state[k] = state[k] + first_weight * round_ext(nt, 3, k) + second_weight * round_ext(nt, 4, k)
            layers(advance)
            sent(halo_z)
            sent(halo_u)

        @pl.when(nt == NEWTON - 1)
        def _():
            def finish(k):
                out[k] = (state[k][8:16, :128] + first_weight[:, :128] * z0[k]
                          + second_weight[:, :128] * msg[nt, 4, k])
            layers(finish)
        sent(operator)
        sent(sums)
        return carry

    lax.fori_loop(0, NEWTON, newton, 0)


def on_device(gxn, gyn, *args):
    depth = args[0].shape[0]

    def vmem(*shape):
        return pltpu.VMEM(shape, jnp.float32)

    def dma(*shape):
        return pltpu.SemaphoreType.DMA(shape)

    ext = vmem(depth, ROWS, LANES)
    flat = ROWS * depth + 16
    level = vmem(8, 2, flat, 128)
    n0 = depth + 1
    assert n0 <= 16
    scratch = [ext] * 7 + [vmem(ROWS, LANES), ext, ext]
    scratch += [level, level] + [vmem(2, flat, 128)] * 7 + [vmem(depth, *TILE)]
    scratch += [pltpu.VMEM((depth,) + TILE, jnp.int32)] + [pltpu.SMEM(item.shape, jnp.float32) for item in args[4:]]
    scratch += [
        vmem(depth, *TILE), vmem(3, n0, *TILE), vmem(3, n0, *TILE), vmem(3, n0, *TILE),
        vmem(3, 2, 1, *TILE), vmem(3, 1, ROWS, 128), vmem(3, 1, ROWS, 128),
        vmem(NEWTON, HALO, depth, *TILE), vmem(NEWTON, HALO, depth, *TILE), vmem(NEWTON, HALO, depth, *TILE),
        vmem(NEWTON, HALO, 2, 1, *TILE), vmem(NEWTON, HALO, 1, ROWS, 128), vmem(NEWTON, HALO, 1, ROWS, 128),
        vmem(NEWTON, 4, *TILE), vmem(NEWTON, 3, gyn, 4, *TILE), vmem(NEWTON, 2, *TILE), vmem(NEWTON, 2, 3, gyn, *TILE),
        vmem(8, ROWS, 128 * gyn), vmem(ROWS, 128), vmem(gyn, ROWS, 128),
        vmem(NEWTON, 1, 128), vmem(NEWTON, gxn * gyn, 1, 128),
        dma(8), dma(3, 8), dma(3, 8), dma(NEWTON, HALO, 8), dma(NEWTON, HALO, 8),
        dma(NEWTON, 3, gyn), dma(NEWTON, 3, gyn), dma(NEWTON, 2, 3, gyn), dma(NEWTON, 2, 3, gyn),
        dma(NEWTON, gxn, gyn), dma(NEWTON, gxn, gyn),
    ]
    return pl.pallas_call(
        functools.partial(kernel, gxn, gyn, depth),
        out_shape=jax.ShapeDtypeStruct(args[0].shape, jnp.float32),
        in_specs=[pl.BlockSpec(memory_space=pltpu.HBM)] * 8,
        out_specs=pl.BlockSpec(memory_space=pltpu.VMEM),
        scratch_shapes=scratch,
        compiler_params=pltpu.CompilerParams(
            collective_id=0, has_side_effects=True, vmem_limit_bytes=64 * 1024 * 1024),
    )(*args)


def solution(mesh):
    cells = P(None, "gx", "gy")
    placed = (cells, cells, cells, P("gx", "gy"), P(), P(), P(), P())
    return jax.shard_map(
        functools.partial(on_device, mesh.shape["gx"], mesh.shape["gy"]),
        mesh=mesh, in_specs=placed, out_specs=cells, check_vma=False,
    )
```
